32 devices in a mesh: dp: 16 (over z, x, core), split: 2 (over y).
Axes of the slice: x: 2, y: 2, z: 4, core: 2. Of those that a mesh axis runs over, the one named last changes fastest.
Arguments:
- gene_ids: int32 [16, 1024], P('dp'), may hold values from 0 to 7679
- expr_bins: int32 [16, 1024], P('dp'), may hold values from 0 to 50
- gene_order: int32 [16, 1024], P('dp'), may hold values from 0 to 1023, each once within a row
- cell_ids: int32 [16, 2, 512], P('dp'), may hold values from 0 to 3, never falling along the last dimension, each value on 1 to 256 neighbouring positions
- target_bins: int32 [64, 7680], P(None, ('dp', 'split')), may hold values from 0 to 50
- matrices: float32 [9216, 512], P(('dp', 'split'))
- vectors: float32 [3, 6, 512], replicated
- value_table: float32 [51, 512], replicated, may hold values from -0.75 to 0.75
- gene_table: float32 [7680, 512], P(('dp', 'split'))
- matrices_mom: float32 [9216, 512], P(('dp', 'split'))
- vectors_mom: float32 [3, 6, 512], replicated
- value_mom: float32 [51, 512], replicated
- gene_mom: float32 [7680, 512], P(('dp', 'split'))
- matrices_avg: float32 [9216, 512], P(('dp', 'split'))
- vectors_avg: float32 [3, 6, 512], replicated
- value_avg: float32 [51, 512], replicated, may hold values from -0.75 to 0.75
- gene_avg: float32 [7680, 512], P(('dp', 'split'))
Outputs:
- loss_sum: float32 [], replicated
- grad_norm: float32 [], replicated
- matrices_mom_new: float32 [9216, 512], P(('dp', 'split'))
- matrices_new: float32 [9216, 512], P(('dp', 'split'))
- matrices_avg_new: float32 [9216, 512], P(('dp', 'split'))
- vectors_mom_new: float32 [3, 6, 512], replicated
- vectors_new: float32 [3, 6, 512], replicated
- vectors_avg_new: float32 [3, 6, 512], replicated
- value_mom_new: float32 [51, 512], replicated
- value_new: float32 [51, 512], replicated
- value_avg_new: float32 [51, 512], replicated
- gene_mom_new: float32 [7680, 512], P(('dp', 'split'))
- gene_new: float32 [7680, 512], P(('dp', 'split'))
- gene_avg_new: float32 [7680, 512], P(('dp', 'split'))
The draws below stay inside these ranges and needn't reach their ends.
Inputs may be any that keep to these rules, and one draw needn't show every extreme that they name: Each row of gene_order is a permutation of 0 to 1023. `cell_ids`: along each half of a row the cell numbers never fall; each of the 4 cells holds 1 to 256 positions of each half, and one holds exactly 256.
All inputs are finite; a program needn't handle non-finite values.
Results may differ from the reference program's by a relative error of at most 0.011.
Values may be sent and summed in bfloat16 or wider, within the bound.
No kernel may reach another device: no remote copies, remote signals or barrier semaphores. Data moves between devices by JAX's collectives and lax.ppermute only.
A program may use at most 320 MiB of HBM per device.

```python
import math
import jax
import jax.numpy as jnp
import numpy as np
from jax import lax

D = 512
HEADS = 8
HEAD_DIM = 64
BINS = 51
VOCAB = 7680
LAYERS = 3
HALF = 512
LEN = 1024
MOST = 256
CELLS_ROW = 4
ROWS = 16
CELLS_ALL = 64
PARAMS = 8686080


def bounded_normal(key, shape):
    return jax.random.truncated_normal(key, -3.0, 3.0, shape, jnp.float32)


def matrix_law(key):
    kinds = jnp.arange(LAYERS * 6 * D) // D % 6
    factor = jnp.where(kinds == 3, 3.0, jnp.where(kinds == 5, 1.5, 1.0)) / math.sqrt(D)
    return bounded_normal(key, (LAYERS * 6 * D, D)) * factor[:, None]


def vector_law(key):
    gain_key, shift_key = jax.random.split(key)
    rising = 0.5 + jnp.arange(D) / D
    gains = rising * jax.random.uniform(gain_key, (LAYERS, 6, D), jnp.float32, 0.8, 1.2)
    shifts = jax.random.uniform(shift_key, (LAYERS, 6, D), jnp.float32, -0.3, 0.3)
    is_gain = (jnp.arange(6) % 2 == 0) & (jnp.arange(6) < 4)
    return jnp.where(is_gain[None, :, None], gains, shifts)


def rising_rows(base, top):
    rising = 1.0 + top * jnp.arange(VOCAB) / (VOCAB - 1)
    return base * rising[:, None] / math.sqrt(D)


def moment_law(key, shape):
    return bounded_normal(key, shape) * (0.25 / math.sqrt(PARAMS))


def draw_matrices(key, part):
    key = jax.random.fold_in(key, 11)
    return matrix_law(key)


def draw_matrices_avg(key, part):
    key = jax.random.fold_in(key, 12)
    return matrix_law(key)


def draw_vectors(key, part):
    key = jax.random.fold_in(key, 13)
    return vector_law(key)


def draw_vectors_avg(key, part):
    key = jax.random.fold_in(key, 14)
    return vector_law(key)


def draw_gene_table(key, part):
    key = jax.random.fold_in(key, 15)
    return rising_rows(bounded_normal(key, (VOCAB, D)), 2.0)


def draw_gene_avg(key, part):
    key = jax.random.fold_in(key, 16)
    return rising_rows(bounded_normal(key, (VOCAB, D)), 2.0)


def draw_matrices_mom(key, part):
    key = jax.random.fold_in(key, 17)
    return moment_law(key, (LAYERS * 6 * D, D))


def draw_vectors_mom(key, part):
    key = jax.random.fold_in(key, 18)
    return moment_law(key, (LAYERS, 6, D))


def draw_value_mom(key, part):
    key = jax.random.fold_in(key, 19)
    return moment_law(key, (BINS, D))


def draw_gene_mom(key, part):
    key = jax.random.fold_in(key, 20)
    return moment_law(key, (VOCAB, D))


def set_ends(array, key, smallest, high):
    dims = array.shape
    spot = [jax.random.randint(jax.random.fold_in(key, axis), (), 0, dims[axis]) for axis in range(len(dims))]
    array = array.at[tuple(spot)].set(smallest)
    longest = dims.index(max(dims))
    spot[longest] = (spot[longest] + 1) % dims[longest]
    return array.at[tuple(spot)].set(high)


def profile(amount, total, bound, skew):
    portions = [(1 << 20) // math.isqrt(rank ** skew) + 1 for rank in range(2, amount + 1)]
    rest, holding = total - bound - (amount - 1), [1] * (amount - 1)
    while rest > 0:
        movable = [i for i in range(amount - 1) if holding[i] < bound]
        mass, budget = sum([portions[i] for i in movable]), rest
        for i in movable:
            extra = min(bound - holding[i], max(1, budget * portions[i] // mass), rest)
            holding[i] = holding[i] + extra
            rest = rest - extra
    return np.array([bound] + holding)


def uneven_parts(stream_key, amount, total, bound, slope):
    if amount == 2:
        one = jax.random.randint(stream_key, (), max(1, total - bound), min(bound, total - 1) + 1)
        return jnp.stack([one, total - one])
    tallies = jnp.asarray(profile(amount, total, bound, slope), jnp.int32)
    twos = (amount - 1) // 2
    giver, receiver = tallies[1:1 + 2 * twos:2], tallies[2:2 + 2 * twos:2]
    room = jnp.minimum(giver - 1, bound - receiver)
    passed = jax.random.randint(jax.random.fold_in(stream_key, 1), (twos,), 0, 1 << 20) % (room + 1)
    tallies = tallies.at[1:1 + 2 * twos:2].set(giver - passed).at[2:2 + 2 * twos:2].set(receiver + passed)
    return tallies[jax.random.permutation(jax.random.fold_in(stream_key, 2), amount)]


def gaussian(key, extent, width, bound, dtype=jnp.bfloat16):
    entries = jax.random.normal(key, extent, jnp.float32) * width
    return jnp.minimum(jnp.maximum(entries, -bound), bound).astype(dtype)


def setup_inputs(seed: int = 0) -> dict:
    seeds = jax.random.split(jax.random.key(seed), 18)
    gene_ids = set_ends(jax.random.randint(seeds[0], (ROWS, LEN), 0, VOCAB), jax.random.fold_in(seeds[0], 1), 0, VOCAB - 1).astype(jnp.int32)
    expr_bins = set_ends(jax.random.randint(seeds[1], (ROWS, LEN), 0, BINS), jax.random.fold_in(seeds[1], 1), 0, BINS - 1).astype(jnp.int32)
    gene_order = jax.vmap(lambda own: jax.random.permutation(own, LEN))(jax.random.split(seeds[2], ROWS)).reshape((ROWS, LEN)).astype(jnp.int32)
    cell_ids = jax.vmap(lambda own: jnp.searchsorted(jnp.cumsum(uneven_parts(own, CELLS_ROW, HALF, MOST, 0)), jnp.arange(HALF), side="right"))(jax.random.split(seeds[3], ROWS * 2)).reshape((ROWS, 2, HALF)).astype(jnp.int32)
    target_bins = set_ends(jax.random.randint(seeds[4], (CELLS_ALL, VOCAB), 0, BINS), jax.random.fold_in(seeds[4], 1), 0, BINS - 1).astype(jnp.int32)
    matrices = draw_matrices(jax.random.fold_in(seeds[17], 71), 0)
    vectors = draw_vectors(jax.random.fold_in(seeds[17], 71), 0)
    value_table = gaussian(seeds[7], (BINS, D), 0.05, 0.75, jnp.float32)
    gene_table = draw_gene_table(jax.random.fold_in(seeds[17], 71), 0)
    matrices_mom = draw_matrices_mom(jax.random.fold_in(seeds[17], 71), 0)
    vectors_mom = draw_vectors_mom(jax.random.fold_in(seeds[17], 71), 0)
    value_mom = draw_value_mom(jax.random.fold_in(seeds[17], 71), 0)
    gene_mom = draw_gene_mom(jax.random.fold_in(seeds[17], 71), 0)
    matrices_avg = draw_matrices_avg(jax.random.fold_in(seeds[17], 71), 0)
    vectors_avg = draw_vectors_avg(jax.random.fold_in(seeds[17], 71), 0)
    value_avg = gaussian(seeds[15], (BINS, D), 0.05, 0.75, jnp.float32)
    gene_avg = draw_gene_avg(jax.random.fold_in(seeds[17], 71), 0)
    return {"gene_ids": gene_ids, "expr_bins": expr_bins, "gene_order": gene_order, "cell_ids": cell_ids, "target_bins": target_bins, "matrices": matrices, "vectors": vectors, "value_table": value_table, "gene_table": gene_table, "matrices_mom": matrices_mom, "vectors_mom": vectors_mom, "value_mom": value_mom, "gene_mom": gene_mom, "matrices_avg": matrices_avg, "vectors_avg": vectors_avg, "value_avg": value_avg, "gene_avg": gene_avg}


EPSILON = 1e-05
NEGATIVE = -1e+30
LEARN_RATE = 200.0
MOMENTUM = 0.9
AVERAGE_DECAY = 0.7
CLIP_NORM = 0.25
HIGHEST = lax.Precision.HIGHEST

@jax.custom_vjp
def low(v):
    return lax.optimization_barrier(v.astype(jnp.bfloat16)).astype(jnp.float32)

@jax.custom_vjp
def low_back(v):
    return v

def low_keep(v):
    return (low(v), None)

def low_pass(kept, grad):
    return (grad,)

def back_keep(v):
    return (v, None)

def back_low(kept, grad):
    return (low(grad),)
low.defvjp(low_keep, low_pass)
low_back.defvjp(back_keep, back_low)

def layer_norm(summed, gains, offset):
    average = lax.optimization_barrier(jnp.mean(summed, axis=-1, keepdims=True))
    centered = summed - average
    variance = lax.optimization_barrier(jnp.mean(centered * centered, axis=-1, keepdims=True))
    return centered * lax.rsqrt(variance + EPSILON) * gains + offset

def encode(mats, vectors, cell_all, hidden_state):
    length = hidden_state.shape[0]
    places = jnp.arange(length)
    allowed = (places[None, :] < HALF) & (cell_all[None, :] == cell_all[:, None]) | (places[None, :] == places[:, None])
    scaling = 1.0 / math.sqrt(HEAD_DIM)
    for layer_index in range(LAYERS):
        weight = mats[layer_index]
        vector_row = vectors[layer_index]
        inputs = low(hidden_state)
        projected = jnp.einsum('td,jde->jte', inputs, weight[0:3], precision=HIGHEST)
        projected = low(low_back(projected))
        queries = projected[0].reshape(length, HEADS, HEAD_DIM)
        key_rows = projected[1].reshape(length, HEADS, HEAD_DIM)
        value_rows = projected[2].reshape(length, HEADS, HEAD_DIM)
        scores = jnp.einsum('thc,shc->hts', queries, key_rows, precision=HIGHEST) * scaling
        scores = low_back(scores)
        scores = jnp.where(allowed[None], scores, NEGATIVE)
        row_max = lax.optimization_barrier(jnp.max(scores, axis=-1, keepdims=True))
        exps = jnp.exp(scores - row_max)
        probability = low(exps / lax.optimization_barrier(jnp.sum(exps, axis=-1, keepdims=True)))
        mixture = jnp.einsum('hts,shc->thc', probability, value_rows, precision=HIGHEST).reshape(length, D)
        mixture = low(low_back(mixture))
        branch = low_back(jnp.dot(mixture, weight[3], precision=HIGHEST))
        hidden_state = layer_norm(hidden_state + branch, vector_row[0], vector_row[1])
        hidden = low_back(jnp.dot(low(hidden_state), weight[4], precision=HIGHEST) + vector_row[4])
        activated = low(jax.nn.gelu(hidden, approximate=False))
        branch = low_back(jnp.dot(activated, weight[5], precision=HIGHEST) + vector_row[5])
        hidden_state = layer_norm(hidden_state + branch, vector_row[2], vector_row[3])
    return hidden_state

def row_forward(mats, vectors, value_table, table, row_ids, row_bins, row_order, row_cells):
    gene_pick = jnp.take(row_ids, row_order)
    bin_pick = jnp.take(row_bins, row_order)
    embedded = low_back(jnp.take(table, gene_pick, axis=0))
    hidden_state = math.sqrt(D) * embedded + jnp.take(value_table, bin_pick, axis=0)
    cell_all = jnp.concatenate([row_cells[0], row_cells[1]])
    hidden_state = encode(mats, vectors, cell_all, hidden_state)
    member = (cell_all[None, :] == jnp.arange(CELLS_ROW)[:, None]).astype(jnp.float32)
    cell_sums = jnp.dot(member, hidden_state, precision=HIGHEST)
    return cell_sums / lax.optimization_barrier(jnp.sum(member, axis=1, keepdims=True))

def reference(gene_ids, expr_bins, gene_order, cell_ids, target_bins, matrices, vectors, value_table, gene_table, matrices_mom, vectors_mom, value_mom, gene_mom, matrices_avg, vectors_avg, value_avg, gene_avg):

    def loss_fn(mat_weights, vec_weights, value_weights, gene_weights):
        mats = low(mat_weights).reshape(LAYERS, 6, D, D)
        table = low(gene_weights)
        row_step = jax.checkpoint(row_forward)

        def row_fn(row_data):
            return row_step(mats, vec_weights, value_weights, table, *row_data)
        pooled = lax.map(row_fn, (gene_ids, expr_bins, gene_order, cell_ids))
        cell_rows = low(pooled.reshape(CELLS_ALL, D))
        predicted = low_back(jnp.dot(cell_rows, table.T, precision=HIGHEST))
        target = target_bins.astype(jnp.float32) * (4.0 / (BINS - 1)) - 2.0
        errors = predicted - target
        total_error = jnp.sum(errors * errors)
        return (total_error / VOCAB, total_error)
    weights = (matrices, vectors, value_table, gene_table)
    loss_value, pullback, loss_sum = jax.vjp(loss_fn, *weights, has_aux=True)
    gradients = pullback(jnp.ones_like(loss_value))
    squares = jnp.sum(gradients[0] * gradients[0]) + jnp.sum(gradients[1] * gradients[1])
    squares = squares + jnp.sum(gradients[2] * gradients[2]) + jnp.sum(gradients[3] * gradients[3])
    grad_norm = jnp.sqrt(squares)
    factor = CLIP_NORM / grad_norm

    def update(weight, moment, average, gradient):
        clipped = factor * gradient
        moment_new = MOMENTUM * moment + clipped
        weight_new = weight - LEARN_RATE * (clipped + MOMENTUM * moment_new)
        return (moment_new, weight_new, AVERAGE_DECAY * average + (1.0 - AVERAGE_DECAY) * weight_new)
    mat_out = update(matrices, matrices_mom, matrices_avg, gradients[0])
    vec_out = update(vectors, vectors_mom, vectors_avg, gradients[1])
    value_out = update(value_table, value_mom, value_avg, gradients[2])
    gene_out = update(gene_table, gene_mom, gene_avg, gradients[3])
    return (loss_sum, grad_norm, mat_out[0], mat_out[1], mat_out[2], vec_out[0], vec_out[1], vec_out[2], value_out[0], value_out[1], value_out[2], gene_out[0], gene_out[1], gene_out[2])
```

```python
import math

import jax
import jax.numpy as jnp
from jax import lax
from jax.sharding import Mesh, PartitionSpec as P

D = 512
HEADS = 8
HEAD_DIM = 64
BINS = 51
LAYERS = 3
CELLS_ROW = 4

EPSILON = 1e-05
NEGATIVE = -1e30
LEARN_RATE = 200.0
MOMENTUM = 0.9
AVERAGE_DECAY = 0.7
CLIP_NORM = 0.25
HIGHEST = lax.Precision.HIGHEST
SCALING = 1.0 / math.sqrt(HEAD_DIM)
F32 = jnp.float32
BF16 = jnp.bfloat16


def flip(block, axis):
    return lax.ppermute(block, axis, [(0, 1), (1, 0)])


def ordered(own, other, bit, axis=0):
    low = jnp.where(bit == 0, own, other)
    high = jnp.where(bit == 0, other, own)
    return jnp.stack([low, high], axis=axis)


def short_z(planes):
    return planes in (2, 4)


def slot_of(plane, z, planes):
    return plane ^ z if short_z(planes) else plane


def z_gather(block, planes):
    if not short_z(planes):
        return lax.all_gather(block, "z")
    got = [block]
    for k in range(1, planes):
        got.append(lax.ppermute(block, "z", [(i, i ^ k) for i in range(planes)]))
    return jnp.stack(got)


def z_exchange(blocks, planes):
    if not short_z(planes):
        return lax.all_to_all(blocks, "z", 0, 0)
    got = [blocks[0]]
    for k in range(1, planes):
        got.append(lax.ppermute(blocks[k], "z", [(i, i ^ k) for i in range(planes)]))
    return jnp.stack(got)


def xy_gather(block, cut_axis):
    first, second = jnp.split(block, 2, axis=cut_axis)
    first = jnp.stack([first, flip(first, "x")])
    second = jnp.stack([second, flip(second, "y")])
    first = jnp.stack([first, flip(first, "y")], axis=1)
    second = jnp.stack([second, flip(second, "x")], axis=0)
    return jnp.concatenate([first, second], axis=cut_axis + 2)


def xy_reduce(blocks, cut_axis):
    first, second = jnp.split(blocks, 2, axis=cut_axis + 2)
    add = lambda a, b: (a.astype(F32) + b.astype(F32)).astype(blocks.dtype)
    first = add(first[0], flip(first[1], "x"))
    second = add(second[:, 0], flip(second[:, 1], "y"))
    first = add(first[0], flip(first[1], "y"))
    second = add(second[0], flip(second[1], "x"))
    return jnp.concatenate([first, second], axis=cut_axis)


def by_distance(blocks, bit, axis):
    return jnp.where(bit == 0, blocks, jnp.flip(blocks, axis))


def all_sum(block, planes):
    block = block + flip(block, "c")
    block = block + flip(block, "x")
    block = block + flip(block, "y")
    if not short_z(planes):
        return lax.psum(block, "z")
    k = 1
    while k < planes:
        block = block + lax.ppermute(block, "z", [(i, i ^ k) for i in range(planes)])
        k *= 2
    return block


def norm_forward(summed, gains, offset):
    average = jnp.mean(summed, axis=-1, keepdims=True)
    centered = summed - average
    scaling = lax.rsqrt(jnp.mean(centered * centered, axis=-1, keepdims=True) + EPSILON)
    normed = centered * scaling
    return (normed * gains + offset, normed, scaling)


def norm_backward(upstream, normed, scaling, gains):
    weighted = upstream * gains
    centered = weighted - jnp.mean(weighted, axis=-1, keepdims=True)
    centered = centered - normed * jnp.mean(weighted * normed, axis=-1, keepdims=True)
    return (centered * scaling, jnp.sum(upstream * normed, axis=0), jnp.sum(upstream, axis=0))


def heads_of(array):
    return array.reshape(array.shape[0], HEADS, HEAD_DIM)


def dot(a, b):
    return jnp.dot(a, b, preferred_element_type=F32)


def dot_tn(a, b):
    return lax.dot_general(a, b, (((0,), (0,)), ((), ())), preferred_element_type=F32)


def dot_nt(a, b):
    return lax.dot_general(a, b, (((1,), (1,)), ((), ())), preferred_element_type=F32)


def scores_of(queries, keys, self_keys, allowed, self_on):
    scores = jnp.einsum("thc,shc->hts", queries, keys, preferred_element_type=F32) * SCALING
    scores = jnp.where(allowed[None], scores, NEGATIVE)
    own = jnp.einsum("thc,thc->ht", queries, self_keys, preferred_element_type=F32) * SCALING
    return (scores, jnp.where(self_on[None], own, NEGATIVE))


def layer_forward(state, mats, vecs, allowed, self_on):
    quarter = state.shape[0] // 2
    inputs = state.astype(BF16)
    queries = dot(inputs, mats[0]).astype(BF16)
    keys = dot(inputs, mats[1]).astype(BF16)
    values = dot(inputs, mats[2]).astype(BF16)
    remote = flip(jnp.concatenate([keys[:quarter], values[:quarter]], axis=1), "c")
    key_rows = jnp.concatenate([keys[:quarter], remote[:, :D]])
    value_rows = jnp.concatenate([values[:quarter], remote[:, D:]])
    scores, own = scores_of(
        heads_of(queries), heads_of(key_rows), heads_of(keys), allowed, self_on
    )
    row_max = jnp.maximum(jnp.max(scores, axis=-1), own)
    exps = jnp.exp(scores - row_max[..., None])
    own = jnp.exp(own - row_max)
    total = jnp.sum(exps, axis=-1) + own
    prob = (exps / total[..., None]).astype(BF16)
    own_prob = (own / total).astype(BF16)
    mixture = jnp.einsum("hts,shc->thc", prob, heads_of(value_rows), preferred_element_type=F32)
    mixture = mixture + own_prob.T[..., None].astype(F32) * heads_of(values).astype(F32)
    mixture = mixture.reshape(state.shape).astype(BF16)
    lse = row_max + jnp.log(total)
    first, normed_one, scale_one = norm_forward(
        state + dot(mixture, mats[3]), vecs[0:1], vecs[1:2]
    )
    first_low = first.astype(BF16)
    hidden = dot(first_low, mats[4]) + vecs[4:5]
    activated = jax.nn.gelu(hidden, approximate=False).astype(BF16)
    out, normed_two, scale_two = norm_forward(
        first + dot(activated, mats[5]) + vecs[5:6], vecs[2:3], vecs[3:4]
    )
    saved = (
        inputs, queries, keys, values, key_rows, value_rows, lse, mixture,
        normed_one, scale_one, first_low, hidden, activated, normed_two, scale_two,
    )
    return (out, saved)


def layer_backward(gradient, mats, vecs, saved, allowed, self_on):
    (
        inputs, queries, keys, values, key_rows, value_rows, lse, mixture,
        normed_one, scale_one, first_low, hidden, activated, normed_two, scale_two,
    ) = saved
    quarter = inputs.shape[0] // 2
    sum_two, gain_two, shift_two = norm_backward(gradient, normed_two, scale_two, vecs[2:3])
    low_two = sum_two.astype(BF16)
    bias_out = jnp.sum(low_two.astype(F32), axis=0)
    w_out = dot_tn(activated, low_two)
    grad_act = dot_nt(low_two, mats[5])
    _, gelu_pull = jax.vjp(lambda h: jax.nn.gelu(h, approximate=False), hidden)
    grad_hidden = gelu_pull(grad_act)[0].astype(BF16)
    bias_in = jnp.sum(grad_hidden.astype(F32), axis=0)
    w_in = dot_tn(first_low, grad_hidden)
    grad_first = sum_two + dot_nt(grad_hidden, mats[4])
    sum_one, gain_one, shift_one = norm_backward(grad_first, normed_one, scale_one, vecs[0:1])
    low_one = sum_one.astype(BF16)
    w_mix = dot_tn(mixture, low_one)
    grad_mix = heads_of(dot_nt(low_one, mats[3]).astype(BF16))
    scores, own = scores_of(
        heads_of(queries), heads_of(key_rows), heads_of(keys), allowed, self_on
    )
    prob = jnp.exp(scores - lse[..., None])
    own_prob = jnp.exp(own - lse)
    grad_prob = jnp.einsum("thc,shc->hts", grad_mix, heads_of(value_rows), preferred_element_type=F32)
    grad_own = jnp.einsum("thc,thc->ht", grad_mix, heads_of(values), preferred_element_type=F32)
    delta = jnp.sum(prob * grad_prob, axis=-1) + own_prob * grad_own
    grad_score = (prob * (grad_prob - delta[..., None])).astype(BF16)
    own_score = (own_prob * (grad_own - delta)).astype(BF16).T[..., None].astype(F32)
    grad_q = jnp.einsum("hts,shc->thc", grad_score, heads_of(key_rows), preferred_element_type=F32)
    grad_q = SCALING * (grad_q + own_score * heads_of(keys).astype(F32))
    grad_k = SCALING * jnp.einsum("hts,thc->shc", grad_score, heads_of(queries), preferred_element_type=F32)
    grad_v = jnp.einsum("hts,thc->shc", prob.astype(BF16), grad_mix, preferred_element_type=F32)
    self_k = SCALING * own_score * heads_of(queries).astype(F32)
    self_v = own_prob.astype(BF16).T[..., None].astype(F32) * grad_mix.astype(F32)
    flat = lambda a: a.reshape(a.shape[0], D)
    grad_q, grad_k, grad_v, self_k, self_v = map(flat, (grad_q, grad_k, grad_v, self_k, self_v))
    remote = flip(
        jnp.concatenate([grad_k[quarter:], grad_v[quarter:]], axis=1).astype(BF16), "c"
    ).astype(F32)
    grad_q = grad_q.astype(BF16)
    grad_k = jnp.concatenate([grad_k[:quarter] + remote[:, :D], self_k[quarter:]]).astype(BF16)
    grad_v = jnp.concatenate([grad_v[:quarter] + remote[:, D:], self_v[quarter:]]).astype(BF16)
    state_grad = sum_one + dot_nt(grad_q, mats[0]) + dot_nt(grad_k, mats[1]) + dot_nt(grad_v, mats[2])
    mat_grads = [
        dot_tn(inputs, grad_q), dot_tn(inputs, grad_k), dot_tn(inputs, grad_v), w_mix, w_in, w_out,
    ]
    vec_grads = jnp.stack([gain_one, shift_one, gain_two, shift_two, bias_in, bias_out])
    return (state_grad, [g.astype(BF16) for g in mat_grads], vec_grads)


def local(
    gene_ids, expr_bins, gene_order, cell_ids, target_bins,
    matrices, vectors, value_table, gene_table,
    matrices_mom, vectors_mom, value_mom, gene_mom,
    matrices_avg, vectors_avg, value_avg, gene_avg,
):
    planes = lax.axis_size("z")
    z, x, c, y = (lax.axis_index(a) for a in ("z", "x", "c", "y"))
    half = cell_ids.shape[2]
    quarter = half // 2
    rows_dev = gene_table.shape[0]
    vocab = rows_dev * planes * 8
    mat_rows = matrices.shape[0]

    table_low = gene_table.astype(BF16)
    plane_cells = 4 * CELLS_ROW
    targets = target_bins.astype(BF16).reshape(planes, plane_cells, rows_dev)
    if short_z(planes):
        slots = jnp.stack([lax.dynamic_index_in_dim(targets, z ^ k, 0, False) for k in range(planes)])
    else:
        slots = targets
    table_z = z_gather(table_low, planes)
    target_z = z_exchange(slots, planes)
    table_col = jnp.stack([table_z, flip(table_z, "c")])
    target_col = jnp.stack([target_z, flip(target_z, "c")])
    table_col = table_col.reshape(-1, D)
    col_rows = table_col.shape[0]
    own_rows = col_rows // 2

    codes = gene_ids[0] * 64 + expr_bins[0]
    mine = jnp.stack([codes, gene_order[0], cell_ids[0].reshape(-1)])
    mine = jnp.where(c == y, mine, flip(mine, "c"))
    codes, order, cells = mine[0], mine[1], mine[2]

    def own_part(array):
        return jnp.concatenate(
            [
                lax.dynamic_slice_in_dim(array, c * quarter, quarter),
                lax.dynamic_slice_in_dim(array, half + c * quarter, quarter),
            ]
        )

    picks = own_part(order)
    own_cells = own_part(cells)
    far_known = lax.dynamic_slice_in_dim(cells, (1 - c) * quarter, quarter)
    key_cells = jnp.concatenate([own_cells[:quarter], far_known])
    tokens = picks.shape[0]
    place = jnp.arange(codes.shape[0])
    code = jnp.sum(jnp.where(picks[:, None] == place[None, :], codes[None, :], 0), axis=1)
    genes, levels = code >> 6, code & 63
    allowed = own_cells[:, None] == key_cells[None, :]
    self_on = jnp.arange(tokens) >= quarter

    plane_genes = xy_gather(genes, 0).reshape(-1)
    owner, inner = plane_genes // rows_dev, plane_genes % rows_dev
    dist = jnp.arange(4).repeat(tokens)
    owner_xy = ((owner >> 2) & 1) * 2 + (owner & 1)
    here = owner_xy == x * 2 + y
    slot = ((owner >> 1) & 1 ^ c) * planes + slot_of(owner >> 3, z, planes)
    index = jnp.where(here, slot * rows_dev + inner, -1)
    hot = (index[:, None] == jnp.arange(col_rows)[None, :]).astype(BF16)
    found = dot(hot, table_col).astype(BF16).reshape(2, 2, tokens, D)
    embedded = xy_reduce(found, 0)
    level_hot = (levels[:, None] == jnp.arange(BINS)[None, :]).astype(F32)
    state = math.sqrt(D) * embedded.astype(F32) + jnp.dot(level_hot, value_table, precision=HIGHEST)

    mats_low = matrices.astype(BF16)
    mats_z = z_gather(mats_low, planes)
    if short_z(planes):
        mats_z = jnp.stack([lax.dynamic_index_in_dim(mats_z, z ^ p, 0, False) for p in range(planes)])
    group = planes // 2
    mats = []
    for g in range(2):
        part = mats_z[g * group : (g + 1) * group]
        part = xy_gather(part, 1)
        part = by_distance(by_distance(part, x, 0), y, 1)
        part = ordered(part, flip(part, "c"), c, 0)
        part = part.transpose(3, 1, 0, 2, 4, 5).reshape(-1, D, D)
        mats += [part[i] for i in range(part.shape[0])]

    saved = []
    for layer in range(LAYERS):
        state, kept = layer_forward(
            state, mats[6 * layer : 6 * layer + 6], vectors[layer], allowed, self_on
        )
        saved.append(kept)

    numbers = jnp.arange(CELLS_ROW)
    member = (own_cells[None, :] == numbers[:, None]).astype(F32)
    counts = jnp.sum((cells[None, :] == numbers[:, None]).astype(F32), axis=1)
    share = jnp.dot(member, state, precision=HIGHEST) / counts[:, None]
    pooled = share + flip(share, "c")
    pooled = ordered(pooled, flip(pooled, "y"), y)
    pooled = ordered(pooled, flip(pooled, "x"), x)
    pooled_low = pooled.reshape(plane_cells, D).astype(BF16)
    target_col = target_col.transpose(2, 0, 1, 3).reshape(plane_cells, col_rows).astype(F32)
    predicted = dot_nt(pooled_low, table_col)
    errors = predicted - (target_col * (4.0 / (BINS - 1)) - 2.0)
    loss_part = jnp.sum(errors[:, :own_rows] * errors[:, :own_rows])
    grad_pred = (errors * (2.0 / vocab)).astype(BF16)
    head_grad = dot_tn(grad_pred[:, :own_rows], pooled_low)
    grad_pooled = dot(grad_pred, table_col).reshape(2, 2, CELLS_ROW, D)
    grad_pooled = by_distance(by_distance(grad_pooled, x, 0), y, 1)
    grad_pooled = grad_pooled[0] + flip(grad_pooled[1], "x")
    grad_pooled = grad_pooled[0] + flip(grad_pooled[1], "y")
    gradient = lax.dot_general(
        member, grad_pooled / counts[:, None], (((0,), (0,)), ((), ())), precision=HIGHEST
    )

    mat_grads = [None] * (6 * LAYERS)
    vec_grads = [None] * LAYERS
    for layer in reversed(range(LAYERS)):
        span = slice(6 * layer, 6 * layer + 6)
        gradient, mat_grads[span], vec_grads[layer] = layer_backward(
            gradient, mats[span], vectors[layer], saved[layer], allowed, self_on
        )

    grad_value = jnp.einsum("tb,td->bd", level_hot, gradient, precision=HIGHEST)
    grad_embedded = (math.sqrt(D) * gradient).astype(BF16)
    grad_plane = xy_gather(grad_embedded, 0).reshape(-1, D)
    grad_col = dot_tn(hot, grad_plane)
    grad_own = grad_col[:own_rows] + flip(grad_col[own_rows:].astype(BF16), "c").astype(F32)
    grad_own = (grad_own + head_grad).astype(BF16).reshape(planes, rows_dev, D)
    grad_table = jnp.sum(z_exchange(grad_own, planes).astype(F32), axis=0)

    blocks = [None, None]
    for g in (1, 0):
        part = jnp.stack(mat_grads[9 * g : 9 * g + 9]).reshape(group, 2, 2, 2, mat_rows, D)
        part = jnp.where(c == 0, part, jnp.flip(part, 2))
        near, far = part[:, :, 0], part[:, :, 1]
        part = (near.astype(F32) + flip(far, "c").astype(F32)).astype(BF16)
        part = by_distance(by_distance(part.transpose(1, 2, 0, 3, 4), x, 0), y, 1)
        blocks[g] = xy_reduce(part, 1)
    blocks = jnp.concatenate(blocks)
    if short_z(planes):
        blocks = jnp.stack([lax.dynamic_index_in_dim(blocks, z ^ k, 0, False) for k in range(planes)])
    grad_matrices = jnp.sum(z_exchange(blocks, planes).astype(F32), axis=0)

    small = all_sum(jnp.concatenate([jnp.concatenate(vec_grads), grad_value]), planes)
    grad_vectors = small[: 6 * LAYERS].reshape(vectors.shape)
    grad_value = small[6 * LAYERS :]
    squares = jnp.sum(grad_matrices * grad_matrices) + jnp.sum(grad_table * grad_table)
    lanes = jnp.arange(128)[None, :]
    sums = jnp.where(lanes == 0, squares, jnp.where(lanes == 1, loss_part, 0.0))
    sums = all_sum(jnp.broadcast_to(sums, (8, 128)), planes)
    loss_sum = sums[0, 1]
    grad_norm = jnp.sqrt(sums[0, 0] + jnp.sum(small * small))
    factor = CLIP_NORM / grad_norm

    def update(weight, moment, average, grad_full):
        clipped = factor * grad_full
        moment_new = MOMENTUM * moment + clipped
        weight_new = weight - LEARN_RATE * (clipped + MOMENTUM * moment_new)
        return (
            moment_new,
            weight_new,
            AVERAGE_DECAY * average + (1.0 - AVERAGE_DECAY) * weight_new,
        )

    return (
        loss_sum,
        grad_norm,
        *update(matrices, matrices_mom, matrices_avg, grad_matrices),
        *update(vectors, vectors_mom, vectors_avg, grad_vectors),
        *update(value_table, value_mom, value_avg, grad_value),
        *update(gene_table, gene_mom, gene_avg, grad_table),
    )


def solution(mesh):
    devices = mesh.devices
    fine = Mesh(devices.reshape(devices.shape[0] // 4, 2, 2, devices.shape[1]), ("z", "x", "c", "y"))
    dp = ("z", "x", "c")
    every = ("z", "x", "c", "y")
    weights = (P(every, None), P(), P(), P(every, None))
    in_specs = (P(dp, None),) * 3 + (P(dp, None, None), P(None, every)) + weights * 3
    out_specs = (P(), P()) + (P(every, None),) * 3 + (P(),) * 6 + (P(every, None),) * 3
    return jax.shard_map(local, mesh=fine, in_specs=in_specs, out_specs=out_specs, check_vma=False)
```

```python
import math

import jax
import jax.numpy as jnp
from jax import lax
from jax.experimental import pallas as pl
from jax.experimental.pallas import tpu as pltpu
from jax.sharding import Mesh, PartitionSpec as P

D = 512
HEADS = 8
HEAD_DIM = 64
BINS = 51
LAYERS = 3
CELLS_ROW = 4
PAIR = 128

EPSILON = 1e-05
NEGATIVE = -1e30
LEARN_RATE = 200.0
MOMENTUM = 0.9
AVERAGE_DECAY = 0.7
CLIP_NORM = 0.25
HIGHEST = lax.Precision.HIGHEST
SCALING = 1.0 / math.sqrt(HEAD_DIM)
F32 = jnp.float32
BF16 = jnp.bfloat16


def flip(block, axis):
    return lax.ppermute(block, axis, [(0, 1), (1, 0)])


def ordered(own, other, bit, axis=0):
    low = jnp.where(bit == 0, own, other)
    high = jnp.where(bit == 0, other, own)
    return jnp.stack([low, high], axis=axis)


def short_z(planes):
    return planes in (2, 4)


def slot_of(plane, z, planes):
    return plane ^ z if short_z(planes) else plane


def z_gather(block, planes):
    if not short_z(planes):
        return lax.all_gather(block, "z")
    got = [block]
    for k in range(1, planes):
        got.append(lax.ppermute(block, "z", [(i, i ^ k) for i in range(planes)]))
    return jnp.stack(got)


def z_exchange(blocks, planes):
    if not short_z(planes):
        return lax.all_to_all(blocks, "z", 0, 0)
    got = [blocks[0]]
    for k in range(1, planes):
        got.append(lax.ppermute(blocks[k], "z", [(i, i ^ k) for i in range(planes)]))
    return jnp.stack(got)


def xy_gather(block, cut_axis):
    first, second = jnp.split(block, 2, axis=cut_axis)
    first = jnp.stack([first, flip(first, "x")])
    second = jnp.stack([second, flip(second, "y")])
    first = jnp.stack([first, flip(first, "y")], axis=1)
    second = jnp.stack([second, flip(second, "x")], axis=0)
    return jnp.concatenate([first, second], axis=cut_axis + 2)


def xy_reduce(blocks, cut_axis):
    first, second = jnp.split(blocks, 2, axis=cut_axis + 2)
    add = lambda a, b: (a.astype(F32) + b.astype(F32)).astype(blocks.dtype)
    first = add(first[0], flip(first[1], "x"))
    second = add(second[:, 0], flip(second[:, 1], "y"))
    first = add(first[0], flip(first[1], "y"))
    second = add(second[0], flip(second[1], "x"))
    return jnp.concatenate([first, second], axis=cut_axis)


def by_distance(blocks, bit, axis):
    return jnp.where(bit == 0, blocks, jnp.flip(blocks, axis))


def all_sum(block, planes):
    block = block + flip(block, "c")
    block = block + flip(block, "x")
    block = block + flip(block, "y")
    if not short_z(planes):
        return lax.psum(block, "z")
    k = 1
    while k < planes:
        block = block + lax.ppermute(block, "z", [(i, i ^ k) for i in range(planes)])
        k *= 2
    return block


LIMIT = 16 * 2**20


def call(body, outs, args, scratch=(), flops=10**9):
    size = lambda a: math.prod(a.shape) * a.dtype.itemsize
    shapes = [jax.ShapeDtypeStruct(*o) for o in outs]
    return pl.pallas_call(
        body,
        out_shape=shapes,
        scratch_shapes=list(scratch),
        compiler_params=pltpu.CompilerParams(vmem_limit_bytes=LIMIT),
        cost_estimate=pl.CostEstimate(
            flops=flops,
            bytes_accessed=sum(map(size, args)) + sum(map(size, shapes)),
            transcendentals=0,
        ),
    )(*args)


def dot(a, b):
    return jnp.dot(a, b, preferred_element_type=F32)


def dot_tn(a, b):
    return lax.dot_general(a, b, (((0,), (0,)), ((), ())), preferred_element_type=F32)


def dot_nt(a, b):
    return lax.dot_general(a, b, (((1,), (1,)), ((), ())), preferred_element_type=F32)


def head_marks(width):
    rows = lax.broadcasted_iota(jnp.int32, (D, width), 0) // HEAD_DIM
    return (rows == lax.broadcasted_iota(jnp.int32, (D, width), 1)).astype(F32)


def lane_marks(side, value):
    lanes = lax.broadcasted_iota(jnp.int32, (1, PAIR), 1) // HEAD_DIM
    return jnp.where(lanes == side, value, 0.0)


def norm(summed):
    average = jnp.mean(summed, axis=-1, keepdims=True)
    centered = summed - average
    scaling = lax.rsqrt(jnp.mean(centered * centered, axis=-1, keepdims=True) + EPSILON)
    return (centered * scaling, scaling)


def norm_pull(weighted, normed, scaling):
    centered = weighted - jnp.mean(weighted, axis=-1, keepdims=True)
    return scaling * (centered - normed * jnp.mean(weighted * normed, axis=-1, keepdims=True))


def project_kernel(x_ref, wq_ref, wk_ref, wv_ref, q_ref, k_ref, v_ref, near_ref):
    quarter = near_ref.shape[0]
    low = x_ref[...].astype(BF16)
    keys = dot(low, wk_ref[...]).astype(BF16)
    values = dot(low, wv_ref[...]).astype(BF16)
    k_ref[...] = keys
    v_ref[...] = values
    near_ref[:, :D] = keys[:quarter]
    near_ref[:, D:] = values[:quarter]
    q_ref[...] = dot(low, wq_ref[...]).astype(BF16)


def join_keys(k_ref, v_ref, far_ref, keys_ref, values_ref):
    quarter = far_ref.shape[0]
    keys_ref[:quarter] = k_ref[:quarter]
    keys_ref[quarter:] = far_ref[:, :D]
    values_ref[:quarter] = v_ref[:quarter]
    values_ref[quarter:] = far_ref[:, D:]


def weigh(marks, array):
    return lax.dot_general(
        marks, array, (((0,), (1,)), ((), ())), preferred_element_type=F32, precision=HIGHEST
    )[:HEADS]


def spread(marks, array):
    return lax.dot_general(
        array.astype(BF16), marks[:, :HEADS].astype(BF16), (((0,), (1,)), ((), ())),
        preferred_element_type=F32,
    )


def forward_kernel(
    x_ref, q_ref, k_ref, v_ref, far_ref, own_row_ref, key_col_ref, wo_ref, w1_ref, w2_ref, vec_ref,
    out_ref, mix_ref, lse_ref, u1_ref, r1_ref, low1_ref, slope_ref, act_ref, u2_ref, r2_ref,
    keys_ref, values_ref, bias_ref, own_ref, wide_ref, turned_ref,
):
    tokens = x_ref.shape[0]
    quarter = far_ref.shape[0]
    far_half = slice(quarter, tokens)
    keys_ref[:quarter] = k_ref[:quarter]
    keys_ref[quarter:] = far_ref[:, :D]
    values_ref[:, :quarter] = v_ref[:quarter].T
    values_ref[:, quarter:] = far_ref[:, D:].T
    bias_ref[...] = jnp.where(key_col_ref[...] == own_row_ref[...], 0.0, NEGATIVE)
    marks = head_marks(PAIR)
    product = q_ref[far_half].astype(F32) * k_ref[far_half].astype(F32) * SCALING
    own_ref[...] = weigh(marks, product)

    def pair_step(pair, carry):
        lanes = pl.ds(pl.multiple_of(pair * PAIR, PAIR), PAIR)
        key_pair = keys_ref[:, lanes]
        q_pair = q_ref[:, lanes]
        for side in range(2):
            head = pl.ds(2 * pair + side, 1)
            scores = dot_nt(key_pair, q_pair * lane_marks(side, SCALING).astype(BF16))
            scores = scores + bias_ref[...]
            top = jnp.max(scores, axis=0, keepdims=True)
            own = own_ref[head, :]
            top = jnp.concatenate([top[:, :quarter], jnp.maximum(top[:, quarter:], own)], axis=1)
            exps = jnp.exp(scores - top)
            own = jnp.exp(own - top[:, quarter:])
            amount = jnp.sum(exps, axis=0, keepdims=True)
            amount = jnp.concatenate([amount[:, :quarter], amount[:, quarter:] + own], axis=1)
            inverse = 1.0 / amount
            own_ref[head, :] = own * inverse[:, quarter:]
            lse_ref[head, :] = top + jnp.log(amount)
            prob = (exps * inverse).astype(BF16)
            part = pl.ds(pl.multiple_of(pair * PAIR + side * HEAD_DIM, HEAD_DIM), HEAD_DIM)
            turned_ref[part, :] = dot(values_ref[part, :], prob)
        return carry

    lax.fori_loop(0, D // PAIR, pair_step, 0)
    wide_ref[...] = turned_ref[...].T
    own_share = spread(marks, own_ref[...]) * v_ref[far_half].astype(F32)
    mix_ref[:quarter] = wide_ref[:quarter].astype(BF16)
    mix_ref[far_half] = (wide_ref[far_half] + own_share).astype(BF16)
    for start in range(0, tokens, quarter):
        rows = slice(start, start + quarter)
        normed, scaling = norm(x_ref[rows] + dot(mix_ref[rows], wo_ref[...]))
        u1_ref[rows] = normed
        r1_ref[rows] = scaling
        first = normed * vec_ref[0:1] + vec_ref[1:2]
        first_low = first.astype(BF16)
        low1_ref[rows] = first_low
        hidden = dot(first_low, w1_ref[...]) + vec_ref[4:5]
        share = 0.5 + 0.5 * lax.erf(hidden * math.sqrt(0.5))
        active = (hidden * share).astype(BF16)
        act_ref[rows] = active
        density = jnp.exp(-0.5 * hidden * hidden) * (1.0 / math.sqrt(2.0 * math.pi))
        slope_ref[rows] = share + hidden * density
        normed, scaling = norm(first + dot(active, w2_ref[...]) + vec_ref[5:6])
        u2_ref[rows] = normed
        r2_ref[rows] = scaling
        out_ref[rows] = normed * vec_ref[2:3] + vec_ref[3:4]


def backward_kernel(
    grad_ref, u2_ref, r2_ref, slope_ref, u1_ref, r1_ref, q_ref, k_ref, v_ref, far_ref, lse_ref,
    own_row_ref, key_col_ref, wo_ref, w1_ref, w2_ref, vec_ref,
    sum1_ref, low2_ref, hid_ref, low1_ref, gq_ref, gk_ref, gv_ref, send_ref, gvec_ref,
    keys_ref, values_ref, bias_ref, gmix_ref, own_p_ref, own_s_ref, turned_ref, wide_ref,
):
    tokens = grad_ref.shape[0]
    quarter = far_ref.shape[0]
    join_keys(k_ref, v_ref, far_ref, keys_ref, values_ref)
    turned_ref[...] = keys_ref[...].T
    bias_ref[...] = jnp.where(key_col_ref[...] == own_row_ref[...], 0.0, NEGATIVE)
    sums = [jnp.zeros((1, D), F32) for _ in range(6)]

    def gather(index, value):
        sums[index] = sums[index] + jnp.sum(value, axis=0, keepdims=True)

    for start in range(0, tokens, quarter):
        rows = slice(start, start + quarter)
        upstream = grad_ref[rows]
        normed = u2_ref[rows]
        gather(2, upstream * normed)
        gather(3, upstream)
        sum_two = norm_pull(upstream * vec_ref[2:3], normed, r2_ref[rows])
        low_two = sum_two.astype(BF16)
        low2_ref[rows] = low_two
        gather(5, low_two.astype(F32))
        hid = (dot_nt(low_two, w2_ref[...]) * slope_ref[rows]).astype(BF16)
        hid_ref[rows] = hid
        gather(4, hid.astype(F32))
        upstream = sum_two + dot_nt(hid, w1_ref[...])
        normed = u1_ref[rows]
        gather(0, upstream * normed)
        gather(1, upstream)
        sum_one = norm_pull(upstream * vec_ref[0:1], normed, r1_ref[rows])
        sum1_ref[rows] = sum_one
        low_one = sum_one.astype(BF16)
        low1_ref[rows] = low_one
        gmix_ref[rows] = dot_nt(low_one, wo_ref[...]).astype(BF16)
    gvec_ref[...] = jnp.concatenate(sums + [jnp.zeros((2, D), F32)])

    marks = head_marks(PAIR)
    far_half = slice(quarter, tokens)
    queries = q_ref[far_half].astype(F32)
    mixed = gmix_ref[far_half].astype(F32)
    product = queries * k_ref[far_half].astype(F32) * SCALING
    own_prob = jnp.exp(weigh(marks, product) - lse_ref[:, far_half])
    own_grad = weigh(marks, mixed * v_ref[far_half].astype(F32))
    own_p_ref[...] = own_prob
    own_s_ref[...] = own_grad

    def pair_step(pair, carry):
        lanes = pl.ds(pl.multiple_of(pair * PAIR, PAIR), PAIR)
        key_pair = keys_ref[:, lanes]
        value_pair = values_ref[:, lanes]
        q_pair = q_ref[:, lanes]
        mix_pair = gmix_ref[:, lanes]
        grad_k = jnp.zeros((tokens, PAIR), F32)
        grad_v = jnp.zeros((tokens, PAIR), F32)
        for side in range(2):
            head = 2 * pair + side
            scaled = q_pair * lane_marks(side, SCALING).astype(BF16)
            mix_side = mix_pair * lane_marks(side, 1.0).astype(BF16)
            lse = lse_ref[pl.ds(head, 1), :]
            prob = jnp.exp(dot_nt(key_pair, scaled) + bias_ref[...] - lse)
            grad_p = dot_nt(value_pair, mix_side)
            delta = jnp.sum(prob * grad_p, axis=0, keepdims=True)
            own_p = own_p_ref[pl.ds(head, 1), :]
            own_g = own_s_ref[pl.ds(head, 1), :]
            delta = jnp.concatenate([delta[:, :quarter], delta[:, quarter:] + own_p * own_g], axis=1)
            own_s_ref[pl.ds(head, 1), :] = own_p * (own_g - delta[:, quarter:])
            grad_s = (prob * (grad_p - delta)).astype(BF16)
            grad_k = grad_k + dot(grad_s, scaled)
            grad_v = grad_v + dot(prob.astype(BF16), mix_side)
            part = pl.ds(pl.multiple_of(pair * PAIR + side * HEAD_DIM, HEAD_DIM), HEAD_DIM)
            wide_ref[part, :] = dot(turned_ref[part, :], grad_s)
        gk_ref[:, lanes] = grad_k
        gv_ref[:, lanes] = grad_v
        return carry

    lax.fori_loop(0, D // PAIR, pair_step, 0)
    send_ref[:, :D] = gk_ref[quarter:].astype(BF16)
    send_ref[:, D:] = gv_ref[quarter:].astype(BF16)
    own_score = spread(marks, own_s_ref[...]) * SCALING
    gv_ref[far_half] = spread(marks, own_p_ref[...]) * mixed
    gk_ref[far_half] = own_score * queries
    grad_q = wide_ref[...].T * SCALING
    gq_ref[:quarter] = grad_q[:quarter].astype(BF16)
    gq_ref[far_half] = (grad_q[far_half] + own_score * k_ref[far_half].astype(F32)).astype(BF16)


def weights_kernel(x_ref, gq_ref, mix_ref, g1_ref, h_ref, gz_ref, act_ref, g2_ref, out_ref):
    out_ref[0] = dot_tn(x_ref[...].astype(BF16), gq_ref[...]).astype(BF16)
    out_ref[1] = dot_tn(mix_ref[...], g1_ref[...]).astype(BF16)
    out_ref[2] = dot_tn(h_ref[...], gz_ref[...]).astype(BF16)
    out_ref[3] = dot_tn(act_ref[...], g2_ref[...]).astype(BF16)


def inputs_kernel(
    x_ref, sum1_ref, gq_ref, gk_ref, gv_ref, got_ref, wq_ref, wk_ref, wv_ref,
    grad_ref, out_ref, low_k_ref, low_v_ref,
):
    quarter = got_ref.shape[0]
    low_k_ref[:quarter] = (gk_ref[:quarter] + got_ref[:, :D].astype(F32)).astype(BF16)
    low_v_ref[:quarter] = (gv_ref[:quarter] + got_ref[:, D:].astype(F32)).astype(BF16)
    low_k_ref[quarter:] = gk_ref[quarter:].astype(BF16)
    low_v_ref[quarter:] = gv_ref[quarter:].astype(BF16)
    grad_ref[...] = (
        sum1_ref[...]
        + dot_nt(gq_ref[...], wq_ref[...])
        + dot_nt(low_k_ref[...], wk_ref[...])
        + dot_nt(low_v_ref[...], wv_ref[...])
    )
    low = x_ref[...].astype(BF16)
    out_ref[0] = dot_tn(low, low_k_ref[...]).astype(BF16)
    out_ref[1] = dot_tn(low, low_v_ref[...]).astype(BF16)


def layer_forward(state, mats, vecs, places):
    tokens = state.shape[0]
    quarter = tokens // 2
    own_col, own_row, key_col, key_row = places
    wide = ((tokens, D), F32)
    slim = ((tokens, D), BF16)
    queries, keys, values, near = call(
        project_kernel, [slim, slim, slim, ((quarter, 2 * D), BF16)], (state, *mats[:3])
    )
    far = flip(near, "c")
    col = ((tokens, 1), F32)
    out, mix, lse, u1, r1, low1, slope, act, u2, r2 = call(
        forward_kernel,
        [wide, slim, ((HEADS, tokens), F32), wide, col, slim, wide, slim, wide, col],
        (state, queries, keys, values, far, own_row, key_col, *mats[3:], vecs),
        [
            pltpu.VMEM((tokens, D), BF16),
            pltpu.VMEM((tokens, D), BF16),
            pltpu.VMEM((tokens, tokens), F32),
            pltpu.VMEM((HEADS, quarter), F32),
            pltpu.VMEM((tokens, D), F32),
            pltpu.VMEM((D, tokens), F32),
        ],
        4 * 10**9,
    )
    return (out, (state, queries, keys, values, far, mix, lse, u1, r1, low1, slope, act, u2, r2))


def layer_backward(gradient, mats, vecs, saved, places):
    state, queries, keys, values, far, mix, lse, u1, r1, low1, slope, act, u2, r2 = saved
    tokens = state.shape[0]
    quarter = tokens // 2
    own_col, own_row, key_col, key_row = places
    wide = ((tokens, D), F32)
    slim = ((tokens, D), BF16)
    sum1, g2, gz, g1, gq, gk, gv, send, gvec = call(
        backward_kernel,
        [wide, slim, slim, slim, slim, wide, wide, ((quarter, 2 * D), BF16), ((8, D), F32)],
        (gradient, u2, r2, slope, u1, r1, queries, keys, values, far, lse, own_row, key_col, *mats[3:], vecs),
        [
            pltpu.VMEM((tokens, D), BF16),
            pltpu.VMEM((tokens, D), BF16),
            pltpu.VMEM((tokens, tokens), F32),
            pltpu.VMEM((tokens, D), BF16),
            pltpu.VMEM((HEADS, quarter), F32),
            pltpu.VMEM((HEADS, quarter), F32),
            pltpu.VMEM((D, tokens), BF16),
            pltpu.VMEM((D, tokens), F32),
        ],
        8 * 10**9,
    )
    got = flip(send, "c")
    (part_one,) = call(
        weights_kernel, [((4, D, D), BF16)], (state, gq, mix, g1, low1, gz, act, g2)
    )
    grad, part_two = call(
        inputs_kernel,
        [wide, ((2, D, D), BF16)],
        (state, sum1, gq, gk, gv, got, *mats[:3]),
        [pltpu.VMEM((tokens, D), BF16), pltpu.VMEM((tokens, D), BF16)],
    )
    mat_grads = [part_one[0], part_two[0], part_two[1], part_one[1], part_one[2], part_one[3]]
    return (grad, mat_grads, gvec[:6])


def local(
    gene_ids, expr_bins, gene_order, cell_ids, target_bins,
    matrices, vectors, value_table, gene_table,
    matrices_mom, vectors_mom, value_mom, gene_mom,
    matrices_avg, vectors_avg, value_avg, gene_avg,
):
    planes = lax.axis_size("z")
    z, x, c, y = (lax.axis_index(a) for a in ("z", "x", "c", "y"))
    half = cell_ids.shape[2]
    quarter = half // 2
    rows_dev = gene_table.shape[0]
    vocab = rows_dev * planes * 8
    mat_rows = matrices.shape[0]

    table_low = gene_table.astype(BF16)
    plane_cells = 4 * CELLS_ROW
    targets = target_bins.astype(BF16).reshape(planes, plane_cells, rows_dev)
    if short_z(planes):
        slots = jnp.stack([lax.dynamic_index_in_dim(targets, z ^ k, 0, False) for k in range(planes)])
    else:
        slots = targets
    table_z = z_gather(table_low, planes)
    target_z = z_exchange(slots, planes)
    table_col = jnp.stack([table_z, flip(table_z, "c")])
    target_col = jnp.stack([target_z, flip(target_z, "c")])
    table_col = table_col.reshape(-1, D)
    col_rows = table_col.shape[0]
    own_rows = col_rows // 2

    codes = gene_ids[0] * 64 + expr_bins[0]
    mine = jnp.stack([codes, gene_order[0], cell_ids[0].reshape(-1)])
    mine = jnp.where(c == y, mine, flip(mine, "c"))
    codes, order, cells = mine[0], mine[1], mine[2]

    def own_part(array):
        return jnp.concatenate(
            [
                lax.dynamic_slice_in_dim(array, c * quarter, quarter),
                lax.dynamic_slice_in_dim(array, half + c * quarter, quarter),
            ]
        )

    picks = own_part(order)
    own_cells = own_part(cells)
    far_known = lax.dynamic_slice_in_dim(cells, (1 - c) * quarter, quarter)
    key_cells = jnp.concatenate([own_cells[:quarter], far_known])
    tokens = picks.shape[0]
    place = jnp.arange(codes.shape[0])
    code = jnp.sum(jnp.where(picks[:, None] == place[None, :], codes[None, :], 0), axis=1)
    genes, levels = code >> 6, code & 63
    places = (own_cells[:, None], own_cells[None, :], key_cells[:, None], key_cells[None, :])

    plane_genes = xy_gather(genes, 0).reshape(-1)
    owner, inner = plane_genes // rows_dev, plane_genes % rows_dev
    dist = jnp.arange(4).repeat(tokens)
    owner_xy = ((owner >> 2) & 1) * 2 + (owner & 1)
    here = owner_xy == x * 2 + y
    slot = ((owner >> 1) & 1 ^ c) * planes + slot_of(owner >> 3, z, planes)
    index = jnp.where(here, slot * rows_dev + inner, -1)
    hot = (index[:, None] == jnp.arange(col_rows)[None, :]).astype(BF16)
    found = dot(hot, table_col).astype(BF16).reshape(2, 2, tokens, D)
    embedded = xy_reduce(found, 0)
    level_hot = (levels[:, None] == jnp.arange(BINS)[None, :]).astype(F32)
    state = math.sqrt(D) * embedded.astype(F32) + jnp.dot(level_hot, value_table, precision=HIGHEST)

    mats_low = matrices.astype(BF16)
    mats_z = z_gather(mats_low, planes)
    if short_z(planes):
        mats_z = jnp.stack([lax.dynamic_index_in_dim(mats_z, z ^ p, 0, False) for p in range(planes)])
    group = planes // 2
    mats = []
    for g in range(2):
        part = mats_z[g * group : (g + 1) * group]
        part = xy_gather(part, 1)
        part = by_distance(by_distance(part, x, 0), y, 1)
        part = ordered(part, flip(part, "c"), c, 0)
        part = part.transpose(3, 1, 0, 2, 4, 5).reshape(-1, D, D)
        mats += [part[i] for i in range(part.shape[0])]

    saved = []
    for layer in range(LAYERS):
        state, kept = layer_forward(
            state, mats[6 * layer : 6 * layer + 6], vectors[layer], places
        )
        saved.append(kept)

    numbers = jnp.arange(CELLS_ROW)
    member = (own_cells[None, :] == numbers[:, None]).astype(F32)
    counts = jnp.sum((cells[None, :] == numbers[:, None]).astype(F32), axis=1)
    share = jnp.dot(member, state, precision=HIGHEST) / counts[:, None]
    pooled = share + flip(share, "c")
    pooled = ordered(pooled, flip(pooled, "y"), y)
    pooled = ordered(pooled, flip(pooled, "x"), x)
    pooled_low = pooled.reshape(plane_cells, D).astype(BF16)
    target_col = target_col.transpose(2, 0, 1, 3).reshape(plane_cells, col_rows).astype(F32)
    predicted = dot_nt(pooled_low, table_col)
    errors = predicted - (target_col * (4.0 / (BINS - 1)) - 2.0)
    loss_part = jnp.sum(errors[:, :own_rows] * errors[:, :own_rows])
    grad_pred = (errors * (2.0 / vocab)).astype(BF16)
    head_grad = dot_tn(grad_pred[:, :own_rows], pooled_low)
    grad_pooled = dot(grad_pred, table_col).reshape(2, 2, CELLS_ROW, D)
    grad_pooled = by_distance(by_distance(grad_pooled, x, 0), y, 1)
    grad_pooled = grad_pooled[0] + flip(grad_pooled[1], "x")
    grad_pooled = grad_pooled[0] + flip(grad_pooled[1], "y")
    gradient = lax.dot_general(
        member, grad_pooled / counts[:, None], (((0,), (0,)), ((), ())), precision=HIGHEST
    )

    mat_grads = [None] * (6 * LAYERS)
    vec_grads = [None] * LAYERS
    for layer in reversed(range(LAYERS)):
        span = slice(6 * layer, 6 * layer + 6)
        gradient, mat_grads[span], vec_grads[layer] = layer_backward(
            gradient, mats[span], vectors[layer], saved[layer], places
        )

    grad_value = jnp.einsum("tb,td->bd", level_hot, gradient, precision=HIGHEST)
    grad_embedded = (math.sqrt(D) * gradient).astype(BF16)
    grad_plane = xy_gather(grad_embedded, 0).reshape(-1, D)
    grad_col = dot_tn(hot, grad_plane)
    grad_own = grad_col[:own_rows] + flip(grad_col[own_rows:].astype(BF16), "c").astype(F32)
    grad_own = (grad_own + head_grad).astype(BF16).reshape(planes, rows_dev, D)
    grad_table = jnp.sum(z_exchange(grad_own, planes).astype(F32), axis=0)

    blocks = [None, None]
    for g in (1, 0):
        part = jnp.stack(mat_grads[9 * g : 9 * g + 9]).reshape(group, 2, 2, 2, mat_rows, D)
        part = jnp.where(c == 0, part, jnp.flip(part, 2))
        near, far = part[:, :, 0], part[:, :, 1]
        part = (near.astype(F32) + flip(far, "c").astype(F32)).astype(BF16)
        part = by_distance(by_distance(part.transpose(1, 2, 0, 3, 4), x, 0), y, 1)
        blocks[g] = xy_reduce(part, 1)
    blocks = jnp.concatenate(blocks)
    if short_z(planes):
        blocks = jnp.stack([lax.dynamic_index_in_dim(blocks, z ^ k, 0, False) for k in range(planes)])
    grad_matrices = jnp.sum(z_exchange(blocks, planes).astype(F32), axis=0)

    small = all_sum(jnp.concatenate([jnp.concatenate(vec_grads), grad_value]), planes)
    grad_vectors = small[: 6 * LAYERS].reshape(vectors.shape)
    grad_value = small[6 * LAYERS :]
    squares = jnp.sum(grad_matrices * grad_matrices) + jnp.sum(grad_table * grad_table)
    lanes = jnp.arange(128)[None, :]
    sums = jnp.where(lanes == 0, squares, jnp.where(lanes == 1, loss_part, 0.0))
    sums = all_sum(jnp.broadcast_to(sums, (8, 128)), planes)
    loss_sum = sums[0, 1]
    grad_norm = jnp.sqrt(sums[0, 0] + jnp.sum(small * small))
    factor = CLIP_NORM / grad_norm

    def update(weight, moment, average, grad_full):
        clipped = factor * grad_full
        moment_new = MOMENTUM * moment + clipped
        weight_new = weight - LEARN_RATE * (clipped + MOMENTUM * moment_new)
        return (
            moment_new,
            weight_new,
            AVERAGE_DECAY * average + (1.0 - AVERAGE_DECAY) * weight_new,
        )

    return (
        loss_sum,
        grad_norm,
        *update(matrices, matrices_mom, matrices_avg, grad_matrices),
        *update(vectors, vectors_mom, vectors_avg, grad_vectors),
        *update(value_table, value_mom, value_avg, grad_value),
        *update(gene_table, gene_mom, gene_avg, grad_table),
    )


def solution(mesh):
    devices = mesh.devices
    fine = Mesh(devices.reshape(devices.shape[0] // 4, 2, 2, devices.shape[1]), ("z", "x", "c", "y"))
    dp = ("z", "x", "c")
    every = ("z", "x", "c", "y")
    weights = (P(every, None), P(), P(), P(every, None))
    in_specs = (P(dp, None),) * 3 + (P(dp, None, None), P(None, every)) + weights * 3
    out_specs = (P(), P()) + (P(every, None),) * 3 + (P(),) * 6 + (P(every, None),) * 3
    return jax.shard_map(local, mesh=fine, in_specs=in_specs, out_specs=out_specs, check_vma=False)
```

```python
from functools import partial
import itertools
import math

import jax
import jax.numpy as jnp
from jax import lax
from jax.experimental import pallas as pl
from jax.experimental.pallas import tpu as pltpu
from jax.sharding import Mesh, PartitionSpec as P

D = 512
HEADS = 8
HEAD_DIM = 64
BINS = 51
LAYERS = 3
CELLS_ROW = 4
PAIR = 128
SLOT = 256

EPSILON = 1e-05
NEGATIVE = -1e30
LEARN_RATE = 200.0
MOMENTUM = 0.9
AVERAGE_DECAY = 0.7
CLIP_NORM = 0.25
HIGHEST = lax.Precision.HIGHEST
SCALING = 1.0 / math.sqrt(HEAD_DIM)
F32 = jnp.float32
BF16 = jnp.bfloat16


def flip(block, axis):
    return lax.ppermute(block, axis, [(0, 1), (1, 0)])


def after(values, *needed):
    values, tree = jax.tree.flatten(values)
    needed = jax.tree.leaves(needed)
    if not needed:
        return tree.unflatten(values)
    anywhere = pl.BlockSpec(memory_space=pl.ANY)
    values = pl.pallas_call(
        lambda *refs: None,
        out_shape=[jax.ShapeDtypeStruct(v.shape, v.dtype) for v in values],
        in_specs=[anywhere] * (len(values) + len(needed)),
        out_specs=[anywhere] * len(values),
        input_output_aliases={i: i for i in range(len(values))},
    )(*values, *needed)
    return tree.unflatten(values)


def ordered(own, other, bit, axis=0):
    low = jnp.where(bit == 0, own, other)
    high = jnp.where(bit == 0, other, own)
    return jnp.stack([low, high], axis=axis)


def pick(pair, bit, axis=0):
    first = lax.index_in_dim(pair, 0, axis, False)
    second = lax.index_in_dim(pair, 1, axis, False)
    return jnp.where(bit == 0, first, second)


def short_z(planes):
    return planes == 4


def slot_of(plane, z, planes):
    return plane ^ z if short_z(planes) else plane


def z_swap(block, k, planes, targets=None):
    pairs = [(p ^ k, p) for p in range(planes) if targets is None or p in targets]
    return lax.ppermute(block, "z", pairs)


def xy_gather(block, cut_axis):
    first, second = jnp.split(block, 2, axis=cut_axis)
    early = (flip(first, "x"), flip(second, "y"))
    first = jnp.stack([first, early[0]])
    second = jnp.stack([second, early[1]])
    first = jnp.stack([first, flip(first, "y")], axis=1)
    second = jnp.stack([second, flip(second, "x")], axis=0)
    return (jnp.concatenate([first, second], axis=cut_axis + 2), early)


def rounded_sum(a, b):
    return (a.astype(F32) + b.astype(F32)).astype(a.dtype)


def xy_reduce(blocks, cut_axis):
    first, second = jnp.split(blocks, 2, axis=cut_axis + 2)
    early = (flip(first[1], "x"), flip(second[:, 1], "y"))
    first = rounded_sum(first[0], early[0])
    second = rounded_sum(second[:, 0], early[1])
    first = rounded_sum(first[0], flip(first[1], "y"))
    second = rounded_sum(second[0], flip(second[1], "x"))
    return (jnp.concatenate([first, second], axis=cut_axis), early)


def by_distance(blocks, bit, axis):
    return jnp.where(bit == 0, blocks, jnp.flip(blocks, axis))


class PlaneGather:
    def __init__(self, block, x, y, c):
        self.block, self.bits = block, (x, y, c)

    def one(self, *needed):
        first, second = after(tuple(jnp.split(self.block, 2, axis=1)), *needed)
        self.early = (flip(first, "x"), flip(second, "y"))
        self.halves = (
            ordered(first, self.early[0], self.bits[0], 1),
            ordered(second, self.early[1], self.bits[1], 1),
        )

    def two(self, *needed):
        first, second = after(self.halves, *needed)
        first = ordered(first, flip(first, "y"), self.bits[1], 2)
        second = ordered(second, flip(second, "x"), self.bits[0], 1)
        self.block = jnp.concatenate([first, second], axis=3)

    def three(self, base, store, *needed):
        block = after(self.block, *needed)
        count = 2 * block.size // (D * D)
        return call(
            partial(join_kernel, base), [], (block, flip(block, "c")), [pltpu.VMEM((D, D), BF16)] * count,
            scalars=(self.bits[2][None],), store=store, fresh=store is None,
        )[-1]


class PlaneReduce:
    def __init__(self, near, far, x, y):
        self.bits = (x, y)
        self.block = rounded_sum(near, flip(far, "c"))

    def one(self, *needed):
        x, y = self.bits
        first, second = jnp.split(self.block, 2, axis=3)
        far = after((pick(first, 1 - x, 1), pick(second, 1 - y, 2)), *needed)
        first = rounded_sum(pick(first, x, 1), flip(far[0], "x"))
        second = rounded_sum(pick(second, y, 2), flip(far[1], "y"))
        self.halves = (first, second)

    def two(self, *needed):
        x, y = self.bits
        first, second = self.halves
        far = after((pick(first, 1 - y, 1), pick(second, 1 - x, 1)), *needed)
        first = rounded_sum(pick(first, y, 1), flip(far[0], "y"))
        second = rounded_sum(pick(second, x, 1), flip(far[1], "x"))
        return jnp.concatenate([first, second], axis=1)


def owner_sum(blocks, group, z, planes):
    if not short_z(planes):
        return jnp.sum(lax.all_to_all(blocks, "z", 0, 0).astype(F32), axis=0)
    odd = z & 1
    held = pick(blocks, odd).astype(F32) + z_swap(pick(blocks, 1 - odd), 1, planes).astype(F32)
    got = z_swap(held.astype(BF16), 2, planes, (2 * group, 2 * group + 1))
    return jnp.where(z >> 1 == group, held, 0.0) + got.astype(F32)


def small_sum(block, x, y, z, planes):
    block = block + flip(block, "c")
    near = [block] + [
        lax.ppermute(block, ("x", "y"), [(i, i ^ k) for i in range(4)]) for k in range(1, 4)
    ]
    near = jnp.stack(near)
    at = lambda stack, i: lax.dynamic_index_in_dim(stack, i, 0, False)
    place = 2 * x + y
    block = sum(at(near, place ^ i) for i in range(4))
    if not short_z(planes):
        return lax.psum(block, "z")
    far = jnp.stack([block] + [z_swap(block, k, planes) for k in range(1, planes)])
    return sum(at(far, z ^ i) for i in range(planes))


def all_sum(block, planes):
    for axis in ("c", "x", "y"):
        block = block + flip(block, axis)
    if not short_z(planes):
        return lax.psum(block, "z")
    k = 1
    while k < planes:
        block = block + z_swap(block, k, planes)
        k *= 2
    return block


LIMIT = 40 * 2**20
COST = 10**9
STORE = 132


class Moves:
    def __init__(self, sources, buffers, fetch_sems, store, save_sems):
        self.copies = [
            pltpu.make_async_copy(source, buffer, fetch_sems.at[i])
            for i, (source, buffer) in enumerate(zip(sources, buffers))
        ]
        for copy in self.copies:
            copy.start()
        self.buffers, self.waiting = buffers, set(range(len(buffers)))
        self.store, self.sems, self.saves = store, save_sems, []

    def get(self, i):
        if i in self.waiting:
            self.copies[i].wait()
            self.waiting.remove(i)
        return self.buffers[i]

    def put(self, square, ref, rows=None):
        target = self.store.at[square]
        if rows is not None:
            target = target.at[rows]
        copy = pltpu.make_async_copy(ref, target, self.sems.at[len(self.saves)])
        copy.start()
        self.saves.append(copy)

    def finish(self):
        for i in sorted(self.waiting):
            self.copies[i].wait()
        for copy in self.saves:
            copy.wait()


def call(body, outs, args, scratch=(), needed=(), scalars=(), fetch=(), store=None, fresh=False):
    needed = jax.tree.leaves(needed)
    saving = fresh or store is not None
    shapes = [jax.ShapeDtypeStruct(*o) for o in outs]
    if saving:
        shapes.append(jax.ShapeDtypeStruct((STORE, D, D), BF16))
    olds = [] if store is None else [store]
    counts = [len(scalars) + len(args), len(fetch), len(needed) + len(olds), len(outs), int(saving)]
    counts += [len(fetch), len(scratch)]

    def kernel(*refs):
        groups, at = [], 0
        for count in counts:
            groups.append(refs[at : at + count])
            at += count
        ins, sources, _, results, target, buffers, spare = groups
        sources = [ref.at[square] for ref, (_, square) in zip(sources, fetch)]
        moves = Moves(sources, buffers, refs[at], target[0] if saving else None, refs[at + 1])
        extra = (moves,) if saving or fetch else ()
        body(*extra, *ins, *results, *spare)
        moves.finish()

    small, anywhere = pl.BlockSpec(memory_space=pltpu.SMEM), pl.BlockSpec(memory_space=pl.ANY)
    near = pl.BlockSpec(memory_space=pltpu.VMEM)
    first = len(scalars) + len(args) + len(fetch) + len(needed)
    return pl.pallas_call(
        kernel,
        out_shape=shapes,
        in_specs=[small] * len(scalars)
        + [near] * len(args)
        + [anywhere] * (len(fetch) + len(needed) + len(olds)),
        out_specs=[near] * len(outs) + [anywhere] * int(saving),
        input_output_aliases={first: len(outs)} if olds else {},
        scratch_shapes=[pltpu.VMEM((D, D), BF16)] * len(fetch)
        + list(scratch)
        + [pltpu.SemaphoreType.DMA((max(1, len(fetch)),)), pltpu.SemaphoreType.DMA((24,))],
        compiler_params=pltpu.CompilerParams(vmem_limit_bytes=LIMIT),
        cost_estimate=pl.CostEstimate(flops=COST, bytes_accessed=COST // 1000, transcendentals=0),
    )(*scalars, *args, *(a for a, _ in fetch), *needed, *olds)


def dot(a, b):
    return jnp.dot(a, b, preferred_element_type=F32)


def dot_tn(a, b):
    return lax.dot_general(a, b, (((0,), (0,)), ((), ())), preferred_element_type=F32)


def dot_nt(a, b):
    return lax.dot_general(a, b, (((1,), (1,)), ((), ())), preferred_element_type=F32)


def head_marks(width):
    rows = lax.broadcasted_iota(jnp.int32, (D, width), 0) // HEAD_DIM
    return (rows == lax.broadcasted_iota(jnp.int32, (D, width), 1)).astype(F32)


def lane_marks(side, value):
    lanes = lax.broadcasted_iota(jnp.int32, (1, PAIR), 1) // HEAD_DIM
    return jnp.where(lanes == side, value, 0.0)


def norm(summed):
    average = jnp.mean(summed, axis=-1, keepdims=True)
    centered = summed - average
    scaling = lax.rsqrt(jnp.mean(centered * centered, axis=-1, keepdims=True) + EPSILON)
    return (centered * scaling, scaling)


def norm_pull(weighted, normed, scaling):
    centered = weighted - jnp.mean(weighted, axis=-1, keepdims=True)
    return scaling * (centered - normed * jnp.mean(weighted * normed, axis=-1, keepdims=True))


def project(low, rows, moves, first, q_ref, k_ref, v_ref, near_ref):
    quarter = near_ref.shape[0]
    keys = dot(low, moves.get(first + 1)[...]).astype(BF16)
    values = dot(low, moves.get(first + 2)[...]).astype(BF16)
    k_ref[rows] = keys
    v_ref[rows] = values
    if rows.start == 0:
        near_ref[:, :D] = keys[:quarter]
        near_ref[:, D:] = values[:quarter]
    q_ref[rows] = dot(low, moves.get(first)[...]).astype(BF16)


def first_kernel(moves, x_ref, q_ref, k_ref, v_ref, near_ref, low_ref):
    low = x_ref[...].astype(BF16)
    low_ref[...] = low
    moves.put(LOW, low_ref)
    rows = slice(0, x_ref.shape[0])
    project(low, rows, moves, 0, q_ref, k_ref, v_ref, near_ref)
    for i, ref in enumerate((q_ref, k_ref, v_ref)):
        moves.put(LOW + 1 + i, ref)


def weigh(marks, array):
    return lax.dot_general(
        marks, array, (((0,), (1,)), ((), ())), preferred_element_type=F32, precision=HIGHEST
    )[:HEADS]


def spread(marks, array):
    return lax.dot_general(
        array.astype(BF16), marks[:, :HEADS].astype(BF16), (((0,), (1,)), ((), ())),
        preferred_element_type=F32,
    )


def forward_kernel(last, base, moves, *refs):
    x_ref, q_ref, k_ref, v_ref, far_ref, own_row_ref, key_col_ref, own_col_ref, vec_ref = refs[:9]
    outs, refs = (refs[9:11], refs[11:]) if last else (refs[9:15], refs[15:])
    stat_ref, outs = outs[0], outs[1:]
    mix_ref, u1_ref, low1_ref, slope_ref, act_ref, u2_ref, low_ref = refs[:7]
    keys_ref, values_ref, bias_ref, own_ref, wide_ref, turned_ref, scale_ref = refs[7:]
    moves.put(base + FAR, far_ref.at[:, :D], slice(0, far_ref.shape[0]))
    moves.put(base + FAR, far_ref.at[:, D:], slice(far_ref.shape[0], x_ref.shape[0]))
    tokens = x_ref.shape[0]
    quarter = far_ref.shape[0]
    far_half = slice(quarter, tokens)
    keys_ref[:quarter] = k_ref[:quarter]
    keys_ref[quarter:] = far_ref[:, :D]
    values_ref[:, :quarter] = v_ref[:quarter].T
    values_ref[:, quarter:] = far_ref[:, D:].T
    bias_ref[...] = jnp.where(key_col_ref[...] == own_row_ref[...], 0.0, NEGATIVE)
    marks = head_marks(PAIR)
    product = q_ref[far_half].astype(F32) * k_ref[far_half].astype(F32) * SCALING
    own_ref[...] = weigh(marks, product)

    def pair_step(pair, carry):
        lanes = pl.ds(pl.multiple_of(pair * PAIR, PAIR), PAIR)
        key_pair = keys_ref[:, lanes]
        q_pair = q_ref[:, lanes]
        for side in range(2):
            head = pl.ds(2 * pair + side, 1)
            scores = dot_nt(key_pair, q_pair * lane_marks(side, SCALING).astype(BF16))
            scores = scores + bias_ref[...]
            top = jnp.max(scores, axis=0, keepdims=True)
            own = own_ref[head, :]
            top = jnp.concatenate([top[:, :quarter], jnp.maximum(top[:, quarter:], own)], axis=1)
            exps = jnp.exp(scores - top)
            own = jnp.exp(own - top[:, quarter:])
            amount = jnp.sum(exps, axis=0, keepdims=True)
            amount = jnp.concatenate([amount[:, :quarter], amount[:, quarter:] + own], axis=1)
            inverse = 1.0 / amount
            own_ref[head, :] = own * inverse[:, quarter:]
            stat_ref[head, :] = top + jnp.log(amount)
            prob = (exps * inverse).astype(BF16)
            part = pl.ds(pl.multiple_of(pair * PAIR + side * HEAD_DIM, HEAD_DIM), HEAD_DIM)
            turned_ref[part, :] = dot(values_ref[part, :], prob)
        return carry

    lax.fori_loop(0, D // PAIR, pair_step, 0)
    wide_ref[...] = turned_ref[...].T
    own_share = spread(marks, own_ref[...]) * v_ref[far_half].astype(F32)
    mix_ref[:quarter] = wide_ref[:quarter].astype(BF16)
    mix_ref[far_half] = (wide_ref[far_half] + own_share).astype(BF16)
    moves.put(base + MIX, mix_ref)
    sums = [jnp.zeros((1, D), F32) for _ in range(CELLS_ROW)]
    for start in range(0, tokens, quarter):
        rows = slice(start, start + quarter)
        normed, scaling = norm(x_ref[rows] + dot(mix_ref[rows], moves.get(0)[...]))
        u1_ref[rows] = normed.astype(BF16)
        scale_ref[rows, 0:1] = scaling
        first = normed * vec_ref[0:1] + vec_ref[1:2]
        first_low = first.astype(BF16)
        low1_ref[rows] = first_low
        hidden = dot(first_low, moves.get(1)[...]) + vec_ref[4:5]
        share = 0.5 + 0.5 * lax.erf(hidden * math.sqrt(0.5))
        active = (hidden * share).astype(BF16)
        act_ref[rows] = active
        density = jnp.exp(-0.5 * hidden * hidden) * (1.0 / math.sqrt(2.0 * math.pi))
        slope_ref[rows] = (share + hidden * density).astype(BF16)
        normed, scaling = norm(first + dot(active, moves.get(2)[...]) + vec_ref[5:6])
        u2_ref[rows] = normed.astype(BF16)
        scale_ref[rows, 1:2] = scaling
        state = normed * vec_ref[2:3] + vec_ref[3:4]
        for i, ref in enumerate((u1_ref, low1_ref, slope_ref, act_ref, u2_ref)):
            moves.put(base + U1 + i, ref.at[rows], rows)
        if last:
            for cell in range(CELLS_ROW):
                part = jnp.where(own_col_ref[rows] == cell, state, 0.0)
                sums[cell] = sums[cell] + jnp.sum(part, axis=0, keepdims=True)
        else:
            outs[0][rows] = state
            low = state.astype(BF16)
            low_ref[rows] = low
            project(low, rows, moves, 3, *outs[1:])
    stat_ref[HEADS:] = scale_ref[...].T[:HEADS]
    if last:
        outs[0][...] = jnp.concatenate(sums)
    else:
        for i, ref in enumerate((low_ref, *outs[1:4])):
            moves.put(base + NEXT + i, ref)


def head_kernel(rows_dev, scale, own_rows, pooled_ref, table_ref, target_ref, loss_ref, low_ref, grad_ref):
    table = table_ref[...]
    errors = dot_nt(pooled_ref[...], table) - (target_ref[...] * (4.0 / (BINS - 1)) - 2.0)
    spot = lax.broadcasted_iota(jnp.int32, errors.shape, 1) % SLOT
    errors = jnp.where(spot < rows_dev, errors, 0.0)
    mine = errors[:, :own_rows]
    loss_ref[...] = jnp.broadcast_to(jnp.sum(mine * mine), loss_ref.shape)
    low = (errors * scale).astype(BF16)
    low_ref[...] = low
    grad_ref[...] = dot(low, table)


def backward_kernel(
    seeded, moves,
    grad_ref, own_col_ref, stat_ref, own_row_ref, key_col_ref, vec_ref,
    sum1_ref, low2_ref, hid_ref, low1_ref, gq_ref, gk_ref, gv_ref, send_ref, gvec_ref,
    keys_ref, values_ref, bias_ref, gmix_ref, own_p_ref, own_s_ref, turned_ref, wide_ref, scale_ref,
):
    bias_ref[...] = jnp.where(key_col_ref[...] == own_row_ref[...], 0.0, NEGATIVE)
    scale_ref[...] = stat_ref[HEADS:].T
    u2_ref, w2_ref, slope_ref, w1_ref = (moves.get(i) for i in range(4))
    q_ref = moves.buffers[6]
    lse_ref = stat_ref
    tokens = q_ref.shape[0]
    quarter = tokens // 2
    sums = [jnp.zeros((1, D), F32) for _ in range(6)]

    def gather(index, value):
        sums[index] = sums[index] + jnp.sum(value, axis=0, keepdims=True)

    for start in range(0, tokens, quarter):
        rows = slice(start, start + quarter)
        if seeded:
            upstream = jnp.zeros((quarter, D), F32)
            for cell in range(CELLS_ROW):
                upstream = jnp.where(own_col_ref[rows] == cell, grad_ref[cell : cell + 1], upstream)
        else:
            upstream = grad_ref[rows]
        normed = u2_ref[rows].astype(F32)
        gather(2, upstream * normed)
        gather(3, upstream)
        sum_two = norm_pull(upstream * vec_ref[2:3], normed, scale_ref[rows, 1:2])
        low_two = sum_two.astype(BF16)
        low2_ref[rows] = low_two
        gather(5, low_two.astype(F32))
        hid = (dot_nt(low_two, w2_ref[...]) * slope_ref[rows].astype(F32)).astype(BF16)
        hid_ref[rows] = hid
        gather(4, hid.astype(F32))
        upstream = sum_two + dot_nt(hid, w1_ref[...])
        normed = moves.get(4)[rows].astype(F32)
        gather(0, upstream * normed)
        gather(1, upstream)
        sum_one = norm_pull(upstream * vec_ref[0:1], normed, scale_ref[rows, 0:1])
        sum1_ref[rows] = sum_one
        low_one = sum_one.astype(BF16)
        low1_ref[rows] = low_one
        gmix_ref[rows] = dot_nt(low_one, moves.get(5)[...]).astype(BF16)
    gvec_ref[...] = jnp.concatenate(sums + [jnp.zeros((2, D), F32)])

    q_ref, k_ref, v_ref, far_ref = (moves.get(i) for i in range(6, 10))
    keys_ref[:quarter] = k_ref[:quarter]
    keys_ref[quarter:] = far_ref[:quarter]
    values_ref[:quarter] = v_ref[:quarter]
    values_ref[quarter:] = far_ref[quarter:]
    turned_ref[...] = keys_ref[...].T
    marks = head_marks(PAIR)
    far_half = slice(quarter, tokens)
    queries = q_ref[far_half].astype(F32)
    mixed = gmix_ref[far_half].astype(F32)
    product = queries * k_ref[far_half].astype(F32) * SCALING
    own_prob = jnp.exp(weigh(marks, product) - lse_ref[:HEADS, far_half])
    own_grad = weigh(marks, mixed * v_ref[far_half].astype(F32))
    own_p_ref[...] = own_prob
    own_s_ref[...] = own_grad

    def pair_step(pair, carry):
        lanes = pl.ds(pl.multiple_of(pair * PAIR, PAIR), PAIR)
        key_pair = keys_ref[:, lanes]
        value_pair = values_ref[:, lanes]
        q_pair = q_ref[:, lanes]
        mix_pair = gmix_ref[:, lanes]
        grad_k = jnp.zeros((tokens, PAIR), F32)
        grad_v = jnp.zeros((tokens, PAIR), F32)
        for side in range(2):
            head = 2 * pair + side
            scaled = q_pair * lane_marks(side, SCALING).astype(BF16)
            mix_side = mix_pair * lane_marks(side, 1.0).astype(BF16)
            lse = lse_ref[pl.ds(head, 1), :]
            prob = jnp.exp(dot_nt(key_pair, scaled) + bias_ref[...] - lse)
            grad_p = dot_nt(value_pair, mix_side)
            delta = jnp.sum(prob * grad_p, axis=0, keepdims=True)
            own_p = own_p_ref[pl.ds(head, 1), :]
            own_g = own_s_ref[pl.ds(head, 1), :]
            delta = jnp.concatenate([delta[:, :quarter], delta[:, quarter:] + own_p * own_g], axis=1)
            own_s_ref[pl.ds(head, 1), :] = own_p * (own_g - delta[:, quarter:])
            grad_s = (prob * (grad_p - delta)).astype(BF16)
            grad_k = grad_k + dot(grad_s, scaled)
            grad_v = grad_v + dot(prob.astype(BF16), mix_side)
            part = pl.ds(pl.multiple_of(pair * PAIR + side * HEAD_DIM, HEAD_DIM), HEAD_DIM)
            wide_ref[part, :] = dot(turned_ref[part, :], grad_s)
        gk_ref[:, lanes] = grad_k
        gv_ref[:, lanes] = grad_v
        return carry

    lax.fori_loop(0, D // PAIR, pair_step, 0)
    send_ref[:, :D] = gk_ref[quarter:].astype(BF16)
    send_ref[:, D:] = gv_ref[quarter:].astype(BF16)
    own_score = spread(marks, own_s_ref[...]) * SCALING
    gv_ref[far_half] = spread(marks, own_p_ref[...]) * mixed
    gk_ref[far_half] = own_score * queries
    grad_q = wide_ref[...].T * SCALING
    gq_ref[:quarter] = grad_q[:quarter].astype(BF16)
    gq_ref[far_half] = (grad_q[far_half] + own_score * k_ref[far_half].astype(F32)).astype(BF16)


def weights_kernel(moves, gq_ref, g1_ref, gz_ref, g2_ref, out_ref):
    for i, ref in enumerate((gq_ref, g1_ref, gz_ref, g2_ref)):
        out_ref[i] = dot_tn(moves.get(i)[...], ref[...]).astype(BF16)


def inputs_kernel(
    moves, sum1_ref, gq_ref, gk_ref, gv_ref, got_ref, grad_ref, out_ref, low_k_ref, low_v_ref
):
    quarter = got_ref.shape[0]
    low_k_ref[:quarter] = (gk_ref[:quarter] + got_ref[:, :D].astype(F32)).astype(BF16)
    low_v_ref[:quarter] = (gv_ref[:quarter] + got_ref[:, D:].astype(F32)).astype(BF16)
    low_k_ref[quarter:] = gk_ref[quarter:].astype(BF16)
    low_v_ref[quarter:] = gv_ref[quarter:].astype(BF16)
    grad_ref[...] = (
        sum1_ref[...]
        + dot_nt(gq_ref[...], moves.get(0)[...])
        + dot_nt(low_k_ref[...], moves.get(1)[...])
        + dot_nt(low_v_ref[...], moves.get(2)[...])
    )
    low = moves.get(3)[...]
    out_ref[0] = dot_tn(low, low_k_ref[...]).astype(BF16)
    out_ref[1] = dot_tn(low, low_v_ref[...]).astype(BF16)


def join_kernel(base, moves, c_ref, own_ref, got_ref, *outs):
    count, _, _, rows, _ = own_ref.shape
    mine = c_ref[0] == 0
    for i, (plane, x, c, y) in enumerate(itertools.product(range(count), (0, 1), (0, 1), (0, 1))):
        at, end = rows * i, rows * (i + 1)
        while at < end:
            place, stop = at // D, min(end, (at // D + 1) * D)
            piece = slice(at - rows * i, stop - rows * i)
            own, got = own_ref[plane, x, y, piece], got_ref[plane, x, y, piece]
            chosen = jnp.where(mine, own, got) if c == 0 else jnp.where(mine, got, own)
            outs[place][at - place * D : stop - place * D] = chosen
            at = stop
            if at == place * D + D:
                moves.put(base + place, outs[place])


def split_kernel(plan, c_ref, *refs):
    ins, (near_ref, far_ref) = refs[:-2], refs[-2:]
    count, _, _, rows, _ = near_ref.shape
    mine = c_ref[0] == 0
    at = 0
    for place, index, low, size in plan:
        done = 0
        while done < size:
            i = at // rows
            step = min(size - done, rows * (i + 1) - at)
            plane, x, c, y = i // 8, i // 4 % 2, i // 2 % 2, i % 2
            piece = slice(at - rows * i, at - rows * i + step)
            value = ins[place][index, low + done : low + done + step]
            stays = mine if c == 0 else jnp.logical_not(mine)

            @pl.when(stays)
            def _():
                near_ref[plane, x, y, piece] = value

            @pl.when(jnp.logical_not(stays))
            def _():
                far_ref[plane, x, y, piece] = value

            at, done = at + step, done + step


def shapes_of(tokens):
    return (((tokens, D), F32), ((tokens, D), BF16), ((tokens // 2, 2 * D), BF16))


def vmem(*shape_types):
    return [pltpu.VMEM(*s) for s in shape_types]


SQUARES = 16
LOW, NEXT, FAR, MIX, U1 = 0, 16, 4, 5, 6


def begin(state, mats):
    wide, slim, half = shapes_of(state.shape[0])
    fetch = [(mats, i) for i in range(3)]
    return call(first_kernel, [slim, slim, slim, half], (state,), vmem(slim), fetch=fetch, fresh=True)


def layer_forward(state, queries, keys, values, far, places, vecs, mats, store, layer):
    tokens = state.shape[0]
    wide, slim, half = shapes_of(tokens)
    last = layer == LAYERS - 1
    square = ((tokens, tokens), F32)
    own, turned = ((HEADS, tokens // 2), F32), ((D, tokens), F32)
    outs = [((2 * HEADS, tokens), F32)]
    outs += [((CELLS_ROW, D), F32)] if last else [wide, slim, slim, slim, half]
    own_col, own_row, key_col = places
    return call(
        partial(forward_kernel, last, SQUARES * layer),
        outs,
        (state, queries, keys, values, far, own_row, key_col, own_col, vecs),
        vmem(*[slim] * 7, slim, ((D, tokens), BF16), square, own, wide, turned, ((tokens, PAIR), F32)),
        fetch=[(mats, 6 * layer + i) for i in range(3, 6 if last else 9)],
        store=store,
    )


def layer_backward(gradient, stat, store, places, vecs, mats, layer, needed, more):
    tokens = stat.shape[1]
    wide, slim, half = shapes_of(tokens)
    own_col, own_row, key_col = places
    own, square = ((HEADS, tokens // 2), F32), ((tokens, tokens), F32)
    at, mat = SQUARES * layer, 6 * layer
    saved = lambda *squares: [(store, at + i) for i in squares]
    sum1, g2, gz, g1, gq, gk, gv, send, gvec = call(
        partial(backward_kernel, gradient.shape[0] == CELLS_ROW),
        [wide, slim, slim, slim, slim, wide, wide, half, ((8, D), F32)],
        (gradient, own_col, stat, own_row, key_col, vecs),
        vmem(
            slim, slim, square, slim, own, own, ((D, tokens), BF16), ((D, tokens), F32),
            ((tokens, HEADS), F32),
        ),
        needed,
        fetch=[
            *saved(U1 + 4), (mats, mat + 5), *saved(U1 + 2), (mats, mat + 4), *saved(U1),
            (mats, mat + 3), *saved(LOW + 1, LOW + 2, LOW + 3, FAR),
        ],
    )
    (part_one,) = call(
        weights_kernel,
        [((4, D, D), BF16)],
        (gq, g1, gz, g2),
        fetch=saved(LOW, MIX, U1 + 1, U1 + 3),
    )
    grad, part_two = call(
        inputs_kernel,
        [wide, ((2, D, D), BF16)],
        (sum1, gq, gk, gv, flip(send, "c")),
        vmem(slim, slim),
        more(part_one),
        fetch=[*((mats, mat + i) for i in range(3)), *saved(LOW)],
    )
    parts = [(part_one, 0), (part_two, 0), (part_two, 1), (part_one, 1), (part_one, 2), (part_one, 3)]
    return (grad, parts, gvec[:6])


def split_rows(parts, low, high, count, rows, c):
    arrays, plan = [], []
    for i in range(low // D, -(-high // D)):
        array, index = parts[i]
        known = [j for j, a in enumerate(arrays) if a is array]
        if not known:
            arrays.append(array)
            known = [len(arrays) - 1]
        start, stop = max(low, i * D), min(high, i * D + D)
        plan.append((known[0], index, start - i * D, stop - start))
    half = ((count, 2, 2, rows, D), BF16)
    return call(partial(split_kernel, plan), [half, half], arrays, scalars=(c[None],))


def local(
    gene_ids, expr_bins, gene_order, cell_ids, target_bins,
    matrices, vectors, value_table, gene_table,
    matrices_mom, vectors_mom, value_mom, gene_mom,
    matrices_avg, vectors_avg, value_avg, gene_avg,
):
    planes = lax.axis_size("z")
    short = short_z(planes)
    z, x, c, y = (lax.axis_index(a) for a in ("z", "x", "c", "y"))
    half = cell_ids.shape[2]
    quarter = half // 2
    rows_dev = gene_table.shape[0]
    vocab = rows_dev * planes * 8
    mat_rows = matrices.shape[0]
    plane_cells = 4 * CELLS_ROW

    mats_low = matrices.astype(BF16)
    if short:
        mats_all = [mats_low] + [z_swap(mats_low, k, planes) for k in range(1, planes)]

    codes = gene_ids[0] * 64 + expr_bins[0]
    mine = jnp.stack([codes, gene_order[0], cell_ids[0].reshape(-1)])
    mine = jnp.where(c == y, mine, flip(mine, "c"))
    codes, order, cells = mine[0], mine[1], mine[2]

    def own_part(array):
        return jnp.concatenate(
            [
                lax.dynamic_slice_in_dim(array, c * quarter, quarter),
                lax.dynamic_slice_in_dim(array, half + c * quarter, quarter),
            ]
        )

    picks = own_part(order)
    own_cells = own_part(cells)
    far_known = lax.dynamic_slice_in_dim(cells, (1 - c) * quarter, quarter)
    key_cells = jnp.concatenate([own_cells[:quarter], far_known])
    tokens = picks.shape[0]
    place = jnp.arange(codes.shape[0])
    code = jnp.sum(jnp.where(picks[:, None] == place[None, :], codes[None, :], 0), axis=1)
    genes, levels = code >> 6, code & 63
    places = (own_cells[:, None], own_cells[None, :], key_cells[:, None])
    numbers = jnp.arange(CELLS_ROW)
    counts = jnp.sum((cells[None, :] == numbers[:, None]).astype(F32), axis=1)

    plane_genes = xy_gather(genes, 0)[0].reshape(-1)

    table_low = gene_table.astype(BF16)
    targets = target_bins.astype(BF16).reshape(planes, plane_cells, rows_dev)
    targets = jnp.pad(targets, ((0, 0), (0, 0), (0, D - rows_dev)))
    if short:
        load = lambda k: jnp.concatenate(
            [table_low, lax.dynamic_index_in_dim(targets, z ^ k, 0, False)]
        )
        got = [load(0)] + [z_swap(load(k), k, planes) for k in range(1, planes)]
        slots = jnp.stack(got)
    else:
        rows = lax.all_gather(table_low, "z")
        slots = jnp.concatenate([rows, lax.all_to_all(targets, "z", 0, 0)], axis=1)
        got = [slots]
    table_col = jnp.stack([slots, flip(slots, "c")])
    target_col = table_col[:, :, rows_dev:, :SLOT].transpose(2, 0, 1, 3)
    table_col = table_col.reshape(-1, D)
    col_rows = table_col.shape[0]
    own_rows = col_rows // 2
    target_col = target_col.reshape(plane_cells, col_rows).astype(F32)

    owner, inner = plane_genes // rows_dev, plane_genes % rows_dev
    here = ((owner >> 2) & 1) * 2 + (owner & 1) == x * 2 + y
    slot = ((owner >> 1) & 1 ^ c) * planes + slot_of(owner >> 3, z, planes)
    index = jnp.where(here, slot * SLOT + inner, -1)
    hot = (index[:, None] == jnp.arange(col_rows)[None, :]).astype(BF16)
    found = dot(hot, table_col).astype(BF16).reshape(2, 2, tokens, D)
    embedded, early = xy_reduce(found, 0)
    level_hot = (levels[:, None] == jnp.arange(BINS)[None, :]).astype(F32)
    state = math.sqrt(D) * embedded.astype(F32) + jnp.dot(level_hot, value_table, precision=HIGHEST)

    if short:
        mats_all = jnp.stack(mats_all)
        gathers = []
        for group in range(2):
            part = [
                lax.dynamic_index_in_dim(mats_all, z ^ p, 0, False)
                for p in range(group * planes // 2, (group + 1) * planes // 2)
            ]
            gathers.append(PlaneGather(jnp.stack(part), x, y, c))
        gathers[0].one()
        gathers[0].two()
        gathers[1].one()
        mats = gathers[0].three(0, None)
    else:
        whole = lax.all_gather(mats_low, ("z", "x", "c", "y"), tiled=True).reshape(-1, D, D)
        mats = jnp.concatenate([whole, jnp.zeros((STORE - whole.shape[0], D, D), BF16)])

    queries, keys, values, near, store = begin(state, mats)
    stats = []
    for layer in range(LAYERS):
        far = flip(near, "c")
        if short and layer == 0:
            gathers[1].two()
        if short and layer == 1:
            mats = gathers[1].three(3 * LAYERS, mats)
        stat, *rest, store = layer_forward(
            state, queries, keys, values, far, places, vectors[layer], mats, store, layer
        )
        stats.append(stat)
        if layer < LAYERS - 1:
            state, queries, keys, values, near = rest

    pooled = (rest[0] + flip(rest[0], "c")) / counts[:, None]
    pooled = ordered(pooled, flip(pooled, "y"), y)
    pooled = ordered(pooled, flip(pooled, "x"), x)
    pooled_low = pooled.reshape(plane_cells, D).astype(BF16)
    loss_part, grad_pred, grad_pooled = call(
        partial(head_kernel, rows_dev, 2.0 / vocab, own_rows),
        [((8, 128), F32), ((plane_cells, col_rows), BF16), ((plane_cells, D), F32)],
        (pooled_low, table_col, target_col),
    )
    loss_part = loss_part[0, 0]
    grad_pooled = grad_pooled.reshape(2, 2, CELLS_ROW, D)
    grad_pooled = pick(grad_pooled, x) + flip(pick(grad_pooled, 1 - x), "x")
    grad_pooled = pick(grad_pooled, y) + flip(pick(grad_pooled, 1 - y), "y")
    gradient = grad_pooled / counts[:, None]

    parts = [None] * (6 * LAYERS)
    late = late_blocks = None
    vec_grads = [None] * LAYERS

    def gradients_of(low, high):
        rows = (8 * mat_rows * low, 8 * mat_rows * high)
        return PlaneReduce(*split_rows(parts, *rows, high - low, mat_rows, c), x, y)

    for layer in reversed(range(LAYERS)):
        span = slice(6 * layer, 6 * layer + 6)
        needed, more = (), lambda part: ()
        if short and layer == 1:

            def more(part):
                nonlocal late
                parts[9:12] = [(part, 1), (part, 2), (part, 3)]
                late = gradients_of(planes // 2, planes)
                return ()

        if short and layer == 0:
            late.one()
            needed = late.block
            more = lambda part: late.halves

        gradient, parts[span], vec_grads[layer] = layer_backward(
            gradient, stats[layer], store, places, vectors[layer], mats, layer, needed, more
        )

    grad_value = jnp.einsum("tb,td->bd", level_hot, gradient, precision=HIGHEST)
    grad_embedded = (math.sqrt(D) * gradient).astype(BF16)
    grad_plane, early = xy_gather(grad_embedded, 0)
    rest = gradients_of(0, planes // 2 if short else planes)
    rest.one()
    grad_col = dot_tn(hot, grad_plane.reshape(-1, D))
    grad_own = grad_col[:own_rows] + flip(grad_col[own_rows:].astype(BF16), "c").astype(F32)
    grad_own = grad_own + dot_tn(grad_pred[:, :own_rows], pooled_low)
    grad_own = grad_own.astype(BF16).reshape(planes, SLOT, D)[:, :rows_dev]
    if short:
        swaps = [z_swap(grad_own[k], k, planes) for k in range(1, planes)]
        grad_table = sum(term.astype(F32) for term in [grad_own[0], *swaps])
        blocks = jnp.concatenate([rest.two(grad_own), late.two(grad_own)])
        blocks = [lax.dynamic_index_in_dim(blocks, z ^ k, 0, False) for k in range(planes)]
        terms = [blocks[0]] + [z_swap(blocks[k], k, planes) for k in range(1, planes)]
        grad_matrices = sum(term.astype(F32) for term in terms)
    else:
        swaps = ()
        grad_table = jnp.sum(lax.all_to_all(grad_own, "z", 0, 0).astype(F32), axis=0)
        grad_matrices = owner_sum(rest.two(), 0, z, planes)

    small = jnp.concatenate([jnp.concatenate(vec_grads), grad_value])
    small = all_sum(small, planes)
    grad_vectors = small[: 6 * LAYERS].reshape(vectors.shape)
    grad_value = small[6 * LAYERS :]
    squares = jnp.sum(grad_matrices * grad_matrices) + jnp.sum(grad_table * grad_table)
    lanes = jnp.arange(128)[None, :]
    sums = jnp.where(lanes == 0, squares, jnp.where(lanes == 1, loss_part, 0.0))
    sums = small_sum(jnp.broadcast_to(sums, (8, 128)), x, y, z, planes)
    loss_sum = sums[0, 1]
    grad_norm = jnp.sqrt(sums[0, 0] + jnp.sum(small * small))
    factor = CLIP_NORM / grad_norm

    def update(weight, moment, average, grad_full):
        clipped = factor * grad_full
        moment_new = MOMENTUM * moment + clipped
        weight_new = weight - LEARN_RATE * (clipped + MOMENTUM * moment_new)
        return (
            moment_new,
            weight_new,
            AVERAGE_DECAY * average + (1.0 - AVERAGE_DECAY) * weight_new,
        )

    return (
        loss_sum,
        grad_norm,
        *update(matrices, matrices_mom, matrices_avg, grad_matrices),
        *update(vectors, vectors_mom, vectors_avg, grad_vectors),
        *update(value_table, value_mom, value_avg, grad_value),
        *update(gene_table, gene_mom, gene_avg, grad_table),
    )


def solution(mesh):
    devices = mesh.devices
    fine = Mesh(devices.reshape(devices.shape[0] // 4, 2, 2, devices.shape[1]), ("z", "x", "c", "y"))
    dp = ("z", "x", "c")
    every = ("z", "x", "c", "y")
    weights = (P(every, None), P(), P(), P(every, None))
    in_specs = (P(dp, None),) * 3 + (P(dp, None, None), P(None, every)) + weights * 3
    out_specs = (P(), P()) + (P(every, None),) * 3 + (P(),) * 6 + (P(every, None),) * 3
    return jax.shard_map(local, mesh=fine, in_specs=in_specs, out_specs=out_specs, check_vma=False)
```

```python
from functools import partial
import itertools
import math

import jax
import jax.numpy as jnp
from jax import lax
from jax.experimental import pallas as pl
from jax.experimental.pallas import tpu as pltpu
from jax.sharding import Mesh, PartitionSpec as P

D = 512
HEADS = 8
HEAD_DIM = 64
BINS = 51
LAYERS = 3
CELLS_ROW = 4
PAIR = 128
SLOT = 256

EPSILON = 1e-05
NEGATIVE = -1e30
LEARN_RATE = 200.0
MOMENTUM = 0.9
AVERAGE_DECAY = 0.7
CLIP_NORM = 0.25
HIGHEST = lax.Precision.HIGHEST
SCALING = 1.0 / math.sqrt(HEAD_DIM)
F32 = jnp.float32
BF16 = jnp.bfloat16


def flip(block, axis):
    return lax.ppermute(block, axis, [(0, 1), (1, 0)])


def after(values, *needed):
    values, tree = jax.tree.flatten(values)
    needed = jax.tree.leaves(needed)
    if not needed:
        return tree.unflatten(values)
    anywhere = pl.BlockSpec(memory_space=pl.ANY)
    values = pl.pallas_call(
        lambda *refs: None,
        out_shape=[jax.ShapeDtypeStruct(v.shape, v.dtype) for v in values],
        in_specs=[anywhere] * (len(values) + len(needed)),
        out_specs=[anywhere] * len(values),
        input_output_aliases={i: i for i in range(len(values))},
    )(*values, *needed)
    return tree.unflatten(values)


def ordered(own, other, bit, axis=0):
    low = jnp.where(bit == 0, own, other)
    high = jnp.where(bit == 0, other, own)
    return jnp.stack([low, high], axis=axis)


def pick(pair, bit, axis=0):
    first = lax.index_in_dim(pair, 0, axis, False)
    second = lax.index_in_dim(pair, 1, axis, False)
    return jnp.where(bit == 0, first, second)


def short_z(planes):
    return planes == 4


def slot_of(plane, z, planes):
    return plane ^ z if short_z(planes) else plane


def z_swap(block, k, planes, targets=None):
    pairs = [(p ^ k, p) for p in range(planes) if targets is None or p in targets]
    return lax.ppermute(block, "z", pairs)


def xy_gather(block, cut_axis):
    first, second = jnp.split(block, 2, axis=cut_axis)
    early = (flip(first, "x"), flip(second, "y"))
    first = jnp.stack([first, early[0]])
    second = jnp.stack([second, early[1]])
    first = jnp.stack([first, flip(first, "y")], axis=1)
    second = jnp.stack([second, flip(second, "x")], axis=0)
    return (jnp.concatenate([first, second], axis=cut_axis + 2), early)


def rounded_sum(a, b):
    return (a.astype(F32) + b.astype(F32)).astype(a.dtype)


def xy_reduce(blocks, cut_axis):
    first, second = jnp.split(blocks, 2, axis=cut_axis + 2)
    early = (flip(first[1], "x"), flip(second[:, 1], "y"))
    first = rounded_sum(first[0], early[0])
    second = rounded_sum(second[:, 0], early[1])
    first = rounded_sum(first[0], flip(first[1], "y"))
    second = rounded_sum(second[0], flip(second[1], "x"))
    return (jnp.concatenate([first, second], axis=cut_axis), early)


def by_distance(blocks, bit, axis):
    return jnp.where(bit == 0, blocks, jnp.flip(blocks, axis))


class PlaneGather:
    def __init__(self, block, x, y, c):
        self.block, self.bits = block, (x, y, c)

    def one(self, *needed):
        first, second = after(tuple(jnp.split(self.block, 2, axis=1)), *needed)
        self.early = (flip(first, "x"), flip(second, "y"))
        self.halves = (
            ordered(first, self.early[0], self.bits[0], 1),
            ordered(second, self.early[1], self.bits[1], 1),
        )

    def two(self, *needed):
        first, second = after(self.halves, *needed)
        first = ordered(first, flip(first, "y"), self.bits[1], 2)
        second = ordered(second, flip(second, "x"), self.bits[0], 1)
        self.block = jnp.concatenate([first, second], axis=3)

    def three(self, base, store, *needed):
        block = after(self.block, *needed)
        count = 2 * block.size // (D * D)
        return call(
            partial(join_kernel, base), [], (block, flip(block, "c")), [pltpu.VMEM((D, D), BF16)] * count,
            scalars=(self.bits[2][None],), store=store, fresh=store is None,
        )[-1]


class PlaneReduce:
    def __init__(self, near, far, x, y):
        self.bits = (x, y)
        self.block = rounded_sum(near, flip(far, "c"))

    def one(self, *needed):
        x, y = self.bits
        first, second = jnp.split(self.block, 2, axis=3)
        far = after((pick(first, 1 - x, 1), pick(second, 1 - y, 2)), *needed)
        first = rounded_sum(pick(first, x, 1), flip(far[0], "x"))
        second = rounded_sum(pick(second, y, 2), flip(far[1], "y"))
        self.halves = (first, second)

    def two(self, *needed):
        x, y = self.bits
        first, second = self.halves
        far = after((pick(first, 1 - y, 1), pick(second, 1 - x, 1)), *needed)
        first = rounded_sum(pick(first, y, 1), flip(far[0], "y"))
        second = rounded_sum(pick(second, x, 1), flip(far[1], "x"))
        return jnp.concatenate([first, second], axis=1)


def owner_sum(blocks, group, z, planes):
    if not short_z(planes):
        return jnp.sum(lax.all_to_all(blocks, "z", 0, 0).astype(F32), axis=0)
    odd = z & 1
    held = pick(blocks, odd).astype(F32) + z_swap(pick(blocks, 1 - odd), 1, planes).astype(F32)
    got = z_swap(held.astype(BF16), 2, planes, (2 * group, 2 * group + 1))
    return jnp.where(z >> 1 == group, held, 0.0) + got.astype(F32)


def small_sum(block, x, y, z, planes):
    block = block + flip(block, "c")
    near = [block] + [
        lax.ppermute(block, ("x", "y"), [(i, i ^ k) for i in range(4)]) for k in range(1, 4)
    ]
    near = jnp.stack(near)
    at = lambda stack, i: lax.dynamic_index_in_dim(stack, i, 0, False)
    place = 2 * x + y
    block = sum(at(near, place ^ i) for i in range(4))
    if not short_z(planes):
        return lax.psum(block, "z")
    far = jnp.stack([block] + [z_swap(block, k, planes) for k in range(1, planes)])
    return sum(at(far, z ^ i) for i in range(planes))


def all_sum(block, planes):
    for axis in ("c", "x", "y"):
        block = block + flip(block, axis)
    if not short_z(planes):
        return lax.psum(block, "z")
    k = 1
    while k < planes:
        block = block + z_swap(block, k, planes)
        k *= 2
    return block


LIMIT = 40 * 2**20
COST = 10**9
STORE = 132


class Moves:
    def __init__(self, sources, buffers, fetch_sems, store, save_sems):
        self.copies = [
            pltpu.make_async_copy(source, buffer, fetch_sems.at[i])
            for i, (source, buffer) in enumerate(zip(sources, buffers))
        ]
        for copy in self.copies:
            copy.start()
        self.buffers, self.waiting = buffers, set(range(len(buffers)))
        self.store, self.sems, self.saves = store, save_sems, []

    def get(self, i):
        if i in self.waiting:
            self.copies[i].wait()
            self.waiting.remove(i)
        return self.buffers[i]

    def put(self, square, ref, rows=None):
        target = self.store.at[square]
        if rows is not None:
            target = target.at[rows]
        copy = pltpu.make_async_copy(ref, target, self.sems.at[len(self.saves)])
        copy.start()
        self.saves.append(copy)

    def finish(self):
        for i in sorted(self.waiting):
            self.copies[i].wait()
        for copy in self.saves:
            copy.wait()


def call(body, outs, args, scratch=(), needed=(), scalars=(), fetch=(), store=None, fresh=False):
    needed = jax.tree.leaves(needed)
    saving = fresh or store is not None
    shapes = [jax.ShapeDtypeStruct(*o) for o in outs]
    if saving:
        shapes.append(jax.ShapeDtypeStruct((STORE, D, D), BF16))
    olds = [] if store is None else [store]
    counts = [len(scalars) + len(args), len(fetch), len(needed) + len(olds), len(outs), int(saving)]
    counts += [len(fetch), len(scratch)]

    def kernel(*refs):
        groups, at = [], 0
        for count in counts:
            groups.append(refs[at : at + count])
            at += count
        ins, sources, _, results, target, buffers, spare = groups
        sources = [ref.at[square] for ref, (_, square) in zip(sources, fetch)]
        moves = Moves(sources, buffers, refs[at], target[0] if saving else None, refs[at + 1])
        extra = (moves,) if saving or fetch else ()
        body(*extra, *ins, *results, *spare)
        moves.finish()

    small, anywhere = pl.BlockSpec(memory_space=pltpu.SMEM), pl.BlockSpec(memory_space=pl.ANY)
    near = pl.BlockSpec(memory_space=pltpu.VMEM)
    first = len(scalars) + len(args) + len(fetch) + len(needed)
    return pl.pallas_call(
        kernel,
        out_shape=shapes,
        in_specs=[small] * len(scalars)
        + [near] * len(args)
        + [anywhere] * (len(fetch) + len(needed) + len(olds)),
        out_specs=[near] * len(outs) + [anywhere] * int(saving),
        input_output_aliases={first: len(outs)} if olds else {},
        scratch_shapes=[pltpu.VMEM((D, D), BF16)] * len(fetch)
        + list(scratch)
        + [pltpu.SemaphoreType.DMA((max(1, len(fetch)),)), pltpu.SemaphoreType.DMA((24,))],
        compiler_params=pltpu.CompilerParams(vmem_limit_bytes=LIMIT),
        cost_estimate=pl.CostEstimate(flops=COST, bytes_accessed=COST // 1000, transcendentals=0),
    )(*scalars, *args, *(a for a, _ in fetch), *needed, *olds)


def dot(a, b):
    return jnp.dot(a, b, preferred_element_type=F32)


def dot_tn(a, b):
    return lax.dot_general(a, b, (((0,), (0,)), ((), ())), preferred_element_type=F32)


def dot_nt(a, b):
    return lax.dot_general(a, b, (((1,), (1,)), ((), ())), preferred_element_type=F32)


def head_marks(width):
    rows = lax.broadcasted_iota(jnp.int32, (D, width), 0) // HEAD_DIM
    return (rows == lax.broadcasted_iota(jnp.int32, (D, width), 1)).astype(F32)


def lane_marks(side, value):
    lanes = lax.broadcasted_iota(jnp.int32, (1, PAIR), 1) // HEAD_DIM
    return jnp.where(lanes == side, value, 0.0)


def norm(summed):
    average = jnp.mean(summed, axis=-1, keepdims=True)
    centered = summed - average
    scaling = lax.rsqrt(jnp.mean(centered * centered, axis=-1, keepdims=True) + EPSILON)
    return (centered * scaling, scaling)


def norm_pull(weighted, normed, scaling):
    centered = weighted - jnp.mean(weighted, axis=-1, keepdims=True)
    return scaling * (centered - normed * jnp.mean(weighted * normed, axis=-1, keepdims=True))


def project(low, rows, moves, first, q_ref, k_ref, v_ref, near_ref):
    quarter = near_ref.shape[0]
    keys = dot(low, moves.get(first + 1)[...]).astype(BF16)
    values = dot(low, moves.get(first + 2)[...]).astype(BF16)
    k_ref[rows] = keys
    v_ref[rows] = values
    if rows.start == 0:
        near_ref[:, :D] = keys[:quarter]
        near_ref[:, D:] = values[:quarter]
    q_ref[rows] = dot(low, moves.get(first)[...]).astype(BF16)


def first_kernel(moves, x_ref, q_ref, k_ref, v_ref, near_ref, low_ref):
    low = x_ref[...].astype(BF16)
    low_ref[...] = low
    moves.put(LOW, low_ref)
    rows = slice(0, x_ref.shape[0])
    project(low, rows, moves, 0, q_ref, k_ref, v_ref, near_ref)
    for i, ref in enumerate((q_ref, k_ref, v_ref)):
        moves.put(LOW + 1 + i, ref)


def weigh(marks, array):
    return lax.dot_general(
        marks, array, (((0,), (1,)), ((), ())), preferred_element_type=F32, precision=HIGHEST
    )[:HEADS]


def spread(marks, array):
    return lax.dot_general(
        array.astype(BF16), marks[:, :HEADS].astype(BF16), (((0,), (1,)), ((), ())),
        preferred_element_type=F32,
    )


def forward_kernel(last, base, moves, *refs):
    x_ref, q_ref, k_ref, v_ref, far_ref, own_row_ref, key_col_ref, own_col_ref, vec_ref = refs[:9]
    outs, refs = (refs[9:11], refs[11:]) if last else (refs[9:15], refs[15:])
    stat_ref, outs = outs[0], outs[1:]
    mix_ref, u1_ref, low1_ref, slope_ref, act_ref, u2_ref, low_ref = refs[:7]
    keys_ref, values_ref, bias_ref, own_ref, wide_ref, turned_ref, scale_ref, prob_ref = refs[7:]
    moves.put(base + FAR, far_ref.at[:, :D], slice(0, far_ref.shape[0]))
    moves.put(base + FAR, far_ref.at[:, D:], slice(far_ref.shape[0], x_ref.shape[0]))
    tokens = x_ref.shape[0]
    quarter = far_ref.shape[0]
    far_half = slice(quarter, tokens)
    keys_ref[:quarter] = k_ref[:quarter]
    keys_ref[quarter:] = far_ref[:, :D]
    values_ref[:, :quarter] = v_ref[:quarter].T
    values_ref[:, quarter:] = far_ref[:, D:].T
    bias_ref[...] = jnp.where(key_col_ref[...] == own_row_ref[...], 0.0, NEGATIVE)
    marks = head_marks(PAIR)
    product = q_ref[far_half].astype(F32) * k_ref[far_half].astype(F32) * SCALING
    own_ref[...] = weigh(marks, product)

    def pair_step(pair, carry):
        lanes = slice(pair * PAIR, pair * PAIR + PAIR)
        key_pair = keys_ref[:, lanes]
        q_pair = q_ref[:, lanes]
        for side in range(2):
            head = slice(2 * pair + side, 2 * pair + side + 1)
            scaled = q_pair * lane_marks(side, SCALING).astype(BF16)
            for start in range(0, tokens, 256):
                spots = slice(start, start + 256)
                scores = dot_nt(key_pair, scaled[spots]) + bias_ref[:, spots]
                top = jnp.max(scores, axis=0, keepdims=True)
                if start >= quarter:
                    far_spots = slice(start - quarter, start - quarter + 256)
                    own = own_ref[head, far_spots]
                    top = jnp.maximum(top, own)
                exps = jnp.exp(scores - top)
                amount = jnp.sum(exps, axis=0, keepdims=True)
                if start >= quarter:
                    own = jnp.exp(own - top)
                    amount = amount + own
                inverse = 1.0 / amount
                if start >= quarter:
                    own_ref[head, far_spots] = own * inverse
                stat_ref[head, spots] = top + jnp.log(amount)
                prob_ref[:, spots] = (exps * inverse).astype(BF16)
            part = slice(pair * PAIR + side * HEAD_DIM, pair * PAIR + side * HEAD_DIM + HEAD_DIM)
            turned_ref[part, :] = dot(values_ref[part, :], prob_ref[...])
        return carry

    for pair in range(D // PAIR):
        pair_step(pair, 0)
    wide_ref[...] = turned_ref[...].T
    own_share = spread(marks, own_ref[...]) * v_ref[far_half].astype(F32)
    mix_ref[:quarter] = wide_ref[:quarter].astype(BF16)
    mix_ref[far_half] = (wide_ref[far_half] + own_share).astype(BF16)
    moves.put(base + MIX, mix_ref)
    sums = [jnp.zeros((1, D), F32) for _ in range(CELLS_ROW)]
    for start in range(0, tokens, quarter):
        rows = slice(start, start + quarter)
        normed, scaling = norm(x_ref[rows] + dot(mix_ref[rows], moves.get(0)[...]))
        u1_ref[rows] = normed.astype(BF16)
        scale_ref[rows, 0:1] = scaling
        first = normed * vec_ref[0:1] + vec_ref[1:2]
        first_low = first.astype(BF16)
        low1_ref[rows] = first_low
        hidden = dot(first_low, moves.get(1)[...]) + vec_ref[4:5]
        share = 0.5 + 0.5 * lax.erf(hidden * math.sqrt(0.5))
        active = (hidden * share).astype(BF16)
        act_ref[rows] = active
        density = jnp.exp(-0.5 * hidden * hidden) * (1.0 / math.sqrt(2.0 * math.pi))
        slope_ref[rows] = (share + hidden * density).astype(BF16)
        normed, scaling = norm(first + dot(active, moves.get(2)[...]) + vec_ref[5:6])
        u2_ref[rows] = normed.astype(BF16)
        scale_ref[rows, 1:2] = scaling
        state = normed * vec_ref[2:3] + vec_ref[3:4]
        for i, ref in enumerate((u1_ref, low1_ref, slope_ref, act_ref, u2_ref)):
            moves.put(base + U1 + i, ref.at[rows], rows)
        if last:
            for cell in range(CELLS_ROW):
                part = jnp.where(own_col_ref[rows] == cell, state, 0.0)
                sums[cell] = sums[cell] + jnp.sum(part, axis=0, keepdims=True)
        else:
            outs[0][rows] = state
            low = state.astype(BF16)
            low_ref[rows] = low
            project(low, rows, moves, 3, *outs[1:])
    stat_ref[HEADS:] = scale_ref[...].T[:HEADS]
    if last:
        outs[0][...] = jnp.concatenate(sums)
    else:
        for i, ref in enumerate((low_ref, *outs[1:4])):
            moves.put(base + NEXT + i, ref)


def head_kernel(rows_dev, scale, own_rows, pooled_ref, table_ref, target_ref, loss_ref, low_ref, grad_ref):
    table = table_ref[...]
    errors = dot_nt(pooled_ref[...], table) - (target_ref[...] * (4.0 / (BINS - 1)) - 2.0)
    spot = lax.broadcasted_iota(jnp.int32, errors.shape, 1) % SLOT
    errors = jnp.where(spot < rows_dev, errors, 0.0)
    mine = errors[:, :own_rows]
    loss_ref[...] = jnp.broadcast_to(jnp.sum(mine * mine), loss_ref.shape)
    low = (errors * scale).astype(BF16)
    low_ref[...] = low
    grad_ref[...] = dot(low, table)


def backward_kernel(
    seeded, moves,
    grad_ref, own_col_ref, stat_ref, own_row_ref, key_col_ref, vec_ref,
    sum1_ref, low2_ref, hid_ref, low1_ref, gq_ref, gk_ref, gv_ref, send_ref, gvec_ref,
    keys_ref, values_ref, bias_ref, gmix_ref, own_p_ref, own_s_ref, turned_ref, wide_ref, scale_ref,
    score_ref, prob_ref,
):
    bias_ref[...] = jnp.where(key_col_ref[...] == own_row_ref[...], 0.0, NEGATIVE)
    scale_ref[...] = stat_ref[HEADS:].T
    u2_ref, w2_ref, slope_ref, w1_ref = (moves.get(i) for i in range(4))
    q_ref = moves.buffers[6]
    lse_ref = stat_ref
    tokens = q_ref.shape[0]
    quarter = tokens // 2
    sums = [jnp.zeros((1, D), F32) for _ in range(6)]

    def gather(index, value):
        sums[index] = sums[index] + jnp.sum(value, axis=0, keepdims=True)

    for start in range(0, tokens, quarter):
        rows = slice(start, start + quarter)
        if seeded:
            upstream = jnp.zeros((quarter, D), F32)
            for cell in range(CELLS_ROW):
                upstream = jnp.where(own_col_ref[rows] == cell, grad_ref[cell : cell + 1], upstream)
        else:
            upstream = grad_ref[rows]
        normed = u2_ref[rows].astype(F32)
        gather(2, upstream * normed)
        gather(3, upstream)
        sum_two = norm_pull(upstream * vec_ref[2:3], normed, scale_ref[rows, 1:2])
        low_two = sum_two.astype(BF16)
        low2_ref[rows] = low_two
        gather(5, low_two.astype(F32))
        hid = (dot_nt(low_two, w2_ref[...]) * slope_ref[rows].astype(F32)).astype(BF16)
        hid_ref[rows] = hid
        gather(4, hid.astype(F32))
        upstream = sum_two + dot_nt(hid, w1_ref[...])
        normed = moves.get(4)[rows].astype(F32)
        gather(0, upstream * normed)
        gather(1, upstream)
        sum_one = norm_pull(upstream * vec_ref[0:1], normed, scale_ref[rows, 0:1])
        sum1_ref[rows] = sum_one
        low_one = sum_one.astype(BF16)
        low1_ref[rows] = low_one
        gmix_ref[rows] = dot_nt(low_one, moves.get(5)[...]).astype(BF16)
    gvec_ref[...] = jnp.concatenate(sums + [jnp.zeros((2, D), F32)])

    q_ref, k_ref, v_ref, far_ref = (moves.get(i) for i in range(6, 10))
    keys_ref[:quarter] = k_ref[:quarter]
    keys_ref[quarter:] = far_ref[:quarter]
    values_ref[:quarter] = v_ref[:quarter]
    values_ref[quarter:] = far_ref[quarter:]
    turned_ref[...] = keys_ref[...].T
    marks = head_marks(PAIR)
    far_half = slice(quarter, tokens)
    queries = q_ref[far_half].astype(F32)
    mixed = gmix_ref[far_half].astype(F32)
    product = queries * k_ref[far_half].astype(F32) * SCALING
    own_prob = jnp.exp(weigh(marks, product) - lse_ref[:HEADS, far_half])
    own_grad = weigh(marks, mixed * v_ref[far_half].astype(F32))
    own_p_ref[...] = own_prob
    own_s_ref[...] = own_grad

    def pair_step(pair, carry):
        lanes = slice(pair * PAIR, pair * PAIR + PAIR)
        key_pair = keys_ref[:, lanes]
        value_pair = values_ref[:, lanes]
        q_pair = q_ref[:, lanes]
        mix_pair = gmix_ref[:, lanes]
        grad_k = jnp.zeros((tokens, PAIR), F32)
        grad_v = jnp.zeros((tokens, PAIR), F32)
        for side in range(2):
            head = 2 * pair + side
            scaled = q_pair * lane_marks(side, SCALING).astype(BF16)
            mix_side = mix_pair * lane_marks(side, 1.0).astype(BF16)
            for start in range(0, tokens, 256):
                spots = slice(start, start + 256)
                prob = dot_nt(key_pair, scaled[spots]) + bias_ref[:, spots]
                prob = jnp.exp(prob - lse_ref[slice(head, head + 1), spots])
                grad_p = dot_nt(value_pair, mix_side[spots])
                delta = jnp.sum(prob * grad_p, axis=0, keepdims=True)
                if start >= quarter:
                    far_spots = slice(start - quarter, start - quarter + 256)
                    own_p = own_p_ref[slice(head, head + 1), far_spots]
                    own_g = own_s_ref[slice(head, head + 1), far_spots]
                    delta = delta + own_p * own_g
                    own_s_ref[slice(head, head + 1), far_spots] = own_p * (own_g - delta)
                score_ref[:, spots] = (prob * (grad_p - delta)).astype(BF16)
                prob_ref[:, spots] = prob.astype(BF16)
            grad_s = score_ref[...]
            grad_k = grad_k + dot(grad_s, scaled)
            grad_v = grad_v + dot(prob_ref[...], mix_side)
            part = slice(pair * PAIR + side * HEAD_DIM, pair * PAIR + side * HEAD_DIM + HEAD_DIM)
            wide_ref[part, :] = dot(turned_ref[part, :], grad_s)
        gk_ref[:, lanes] = grad_k
        gv_ref[:, lanes] = grad_v
        return carry

    for pair in range(D // PAIR):
        pair_step(pair, 0)
    send_ref[:, :D] = gk_ref[quarter:].astype(BF16)
    send_ref[:, D:] = gv_ref[quarter:].astype(BF16)
    own_score = spread(marks, own_s_ref[...]) * SCALING
    gv_ref[far_half] = spread(marks, own_p_ref[...]) * mixed
    gk_ref[far_half] = own_score * queries
    grad_q = wide_ref[...].T * SCALING
    gq_ref[:quarter] = grad_q[:quarter].astype(BF16)
    gq_ref[far_half] = (grad_q[far_half] + own_score * k_ref[far_half].astype(F32)).astype(BF16)


def weights_kernel(moves, gq_ref, g1_ref, gz_ref, g2_ref, out_ref):
    for i, ref in enumerate((gq_ref, g1_ref, gz_ref, g2_ref)):
        out_ref[i] = dot_tn(moves.get(i)[...], ref[...]).astype(BF16)


def inputs_kernel(
    moves, sum1_ref, gq_ref, gk_ref, gv_ref, got_ref, grad_ref, out_ref, low_k_ref, low_v_ref
):
    quarter = got_ref.shape[0]
    low_k_ref[:quarter] = (gk_ref[:quarter] + got_ref[:, :D].astype(F32)).astype(BF16)
    low_v_ref[:quarter] = (gv_ref[:quarter] + got_ref[:, D:].astype(F32)).astype(BF16)
    low_k_ref[quarter:] = gk_ref[quarter:].astype(BF16)
    low_v_ref[quarter:] = gv_ref[quarter:].astype(BF16)
    grad_ref[...] = (
        sum1_ref[...]
        + dot_nt(gq_ref[...], moves.get(0)[...])
        + dot_nt(low_k_ref[...], moves.get(1)[...])
        + dot_nt(low_v_ref[...], moves.get(2)[...])
    )
    low = moves.get(3)[...]
    out_ref[0] = dot_tn(low, low_k_ref[...]).astype(BF16)
    out_ref[1] = dot_tn(low, low_v_ref[...]).astype(BF16)


def join_kernel(base, moves, c_ref, own_ref, got_ref, *outs):
    count, _, _, rows, _ = own_ref.shape
    mine = c_ref[0] == 0
    for i, (plane, x, c, y) in enumerate(itertools.product(range(count), (0, 1), (0, 1), (0, 1))):
        at, end = rows * i, rows * (i + 1)
        while at < end:
            place, stop = at // D, min(end, (at // D + 1) * D)
            piece = slice(at - rows * i, stop - rows * i)
            own, got = own_ref[plane, x, y, piece], got_ref[plane, x, y, piece]
            chosen = jnp.where(mine, own, got) if c == 0 else jnp.where(mine, got, own)
            outs[place][at - place * D : stop - place * D] = chosen
            at = stop
            if at == place * D + D:
                moves.put(base + place, outs[place])


def split_kernel(plan, c_ref, *refs):
    ins, (near_ref, far_ref) = refs[:-2], refs[-2:]
    count, _, _, rows, _ = near_ref.shape
    mine = c_ref[0] == 0
    at = 0
    for place, index, low, size in plan:
        done = 0
        while done < size:
            i = at // rows
            step = min(size - done, rows * (i + 1) - at)
            plane, x, c, y = i // 8, i // 4 % 2, i // 2 % 2, i % 2
            piece = slice(at - rows * i, at - rows * i + step)
            value = ins[place][index, low + done : low + done + step]
            stays = mine if c == 0 else jnp.logical_not(mine)

            @pl.when(stays)
            def _():
                near_ref[plane, x, y, piece] = value

            @pl.when(jnp.logical_not(stays))
            def _():
                far_ref[plane, x, y, piece] = value

            at, done = at + step, done + step


def shapes_of(tokens):
    return (((tokens, D), F32), ((tokens, D), BF16), ((tokens // 2, 2 * D), BF16))


def vmem(*shape_types):
    return [pltpu.VMEM(*s) for s in shape_types]


SQUARES = 16
LOW, NEXT, FAR, MIX, U1 = 0, 16, 4, 5, 6


def begin(state, mats):
    wide, slim, half = shapes_of(state.shape[0])
    fetch = [(mats, i) for i in range(3)]
    return call(first_kernel, [slim, slim, slim, half], (state,), vmem(slim), fetch=fetch, fresh=True)


def layer_forward(state, queries, keys, values, far, places, vecs, mats, store, layer):
    tokens = state.shape[0]
    wide, slim, half = shapes_of(tokens)
    last = layer == LAYERS - 1
    square = ((tokens, tokens), F32)
    own, turned = ((HEADS, tokens // 2), F32), ((D, tokens), F32)
    outs = [((2 * HEADS, tokens), F32)]
    outs += [((CELLS_ROW, D), F32)] if last else [wide, slim, slim, slim, half]
    own_col, own_row, key_col = places
    return call(
        partial(forward_kernel, last, SQUARES * layer),
        outs,
        (state, queries, keys, values, far, own_row, key_col, own_col, vecs),
        vmem(*[slim] * 7, slim, ((D, tokens), BF16), square, own, wide, turned, ((tokens, PAIR), F32),
            ((tokens, tokens), BF16)),
        fetch=[(mats, 6 * layer + i) for i in range(3, 6 if last else 9)],
        store=store,
    )


def layer_backward(gradient, stat, store, places, vecs, mats, layer, needed, more):
    tokens = stat.shape[1]
    wide, slim, half = shapes_of(tokens)
    own_col, own_row, key_col = places
    own, square = ((HEADS, tokens // 2), F32), ((tokens, tokens), F32)
    at, mat = SQUARES * layer, 6 * layer
    saved = lambda *squares: [(store, at + i) for i in squares]
    sum1, g2, gz, g1, gq, gk, gv, send, gvec = call(
        partial(backward_kernel, gradient.shape[0] == CELLS_ROW),
        [wide, slim, slim, slim, slim, wide, wide, half, ((8, D), F32)],
        (gradient, own_col, stat, own_row, key_col, vecs),
        vmem(
            slim, slim, square, slim, own, own, ((D, tokens), BF16), ((D, tokens), F32),
            ((tokens, HEADS), F32), ((tokens, tokens), BF16), ((tokens, tokens), BF16),
        ),
        needed,
        fetch=[
            *saved(U1 + 4), (mats, mat + 5), *saved(U1 + 2), (mats, mat + 4), *saved(U1),
            (mats, mat + 3), *saved(LOW + 1, LOW + 2, LOW + 3, FAR),
        ],
    )
    (part_one,) = call(
        weights_kernel,
        [((4, D, D), BF16)],
        (gq, g1, gz, g2),
        fetch=saved(LOW, MIX, U1 + 1, U1 + 3),
    )
    grad, part_two = call(
        inputs_kernel,
        [wide, ((2, D, D), BF16)],
        (sum1, gq, gk, gv, flip(send, "c")),
        vmem(slim, slim),
        more(part_one),
        fetch=[*((mats, mat + i) for i in range(3)), *saved(LOW)],
    )
    parts = [(part_one, 0), (part_two, 0), (part_two, 1), (part_one, 1), (part_one, 2), (part_one, 3)]
    return (grad, parts, gvec[:6])


def split_rows(parts, low, high, count, rows, c):
    arrays, plan = [], []
    for i in range(low // D, -(-high // D)):
        array, index = parts[i]
        known = [j for j, a in enumerate(arrays) if a is array]
        if not known:
            arrays.append(array)
            known = [len(arrays) - 1]
        start, stop = max(low, i * D), min(high, i * D + D)
        plan.append((known[0], index, start - i * D, stop - start))
    half = ((count, 2, 2, rows, D), BF16)
    return call(partial(split_kernel, plan), [half, half], arrays, scalars=(c[None],))


def local(
    gene_ids, expr_bins, gene_order, cell_ids, target_bins,
    matrices, vectors, value_table, gene_table,
    matrices_mom, vectors_mom, value_mom, gene_mom,
    matrices_avg, vectors_avg, value_avg, gene_avg,
):
    planes = lax.axis_size("z")
    short = short_z(planes)
    z, x, c, y = (lax.axis_index(a) for a in ("z", "x", "c", "y"))
    half = cell_ids.shape[2]
    quarter = half // 2
    rows_dev = gene_table.shape[0]
    vocab = rows_dev * planes * 8
    mat_rows = matrices.shape[0]
    plane_cells = 4 * CELLS_ROW

    mats_low = matrices.astype(BF16)
    if short:
        mats_all = [mats_low] + [z_swap(mats_low, k, planes) for k in range(1, planes)]

    codes = gene_ids[0] * 64 + expr_bins[0]
    mine = jnp.stack([codes, gene_order[0], cell_ids[0].reshape(-1)])
    mine = jnp.where(c == y, mine, flip(mine, "c"))
    codes, order, cells = mine[0], mine[1], mine[2]

    def own_part(array):
        return jnp.concatenate(
            [
                lax.dynamic_slice_in_dim(array, c * quarter, quarter),
                lax.dynamic_slice_in_dim(array, half + c * quarter, quarter),
            ]
        )

    picks = own_part(order)
    own_cells = own_part(cells)
    far_known = lax.dynamic_slice_in_dim(cells, (1 - c) * quarter, quarter)
    key_cells = jnp.concatenate([own_cells[:quarter], far_known])
    tokens = picks.shape[0]
    place = jnp.arange(codes.shape[0])
    code = jnp.sum(jnp.where(picks[:, None] == place[None, :], codes[None, :], 0), axis=1)
    genes, levels = code >> 6, code & 63
    places = (own_cells[:, None], own_cells[None, :], key_cells[:, None])
    numbers = jnp.arange(CELLS_ROW)
    counts = jnp.sum((cells[None, :] == numbers[:, None]).astype(F32), axis=1)

    plane_genes = xy_gather(genes, 0)[0].reshape(-1)

    table_low = gene_table.astype(BF16)
    targets = target_bins.astype(BF16).reshape(planes, plane_cells, rows_dev)
    targets = jnp.pad(targets, ((0, 0), (0, 0), (0, D - rows_dev)))
    if short:
        load = lambda k: jnp.concatenate(
            [table_low, lax.dynamic_index_in_dim(targets, z ^ k, 0, False)]
        )
        got = [load(0)] + [z_swap(load(k), k, planes) for k in range(1, planes)]
        slots = jnp.stack(got)
    else:
        rows = lax.all_gather(table_low, "z")
        slots = jnp.concatenate([rows, lax.all_to_all(targets, "z", 0, 0)], axis=1)
        got = [slots]
    table_col = jnp.stack([slots, flip(slots, "c")])
    target_col = table_col[:, :, rows_dev:, :SLOT].transpose(2, 0, 1, 3)
    table_col = table_col.reshape(-1, D)
    col_rows = table_col.shape[0]
    own_rows = col_rows // 2
    target_col = target_col.reshape(plane_cells, col_rows).astype(F32)

    owner, inner = plane_genes // rows_dev, plane_genes % rows_dev
    here = ((owner >> 2) & 1) * 2 + (owner & 1) == x * 2 + y
    slot = ((owner >> 1) & 1 ^ c) * planes + slot_of(owner >> 3, z, planes)
    index = jnp.where(here, slot * SLOT + inner, -1)
    hot = (index[:, None] == jnp.arange(col_rows)[None, :]).astype(BF16)
    found = dot(hot, table_col).astype(BF16).reshape(2, 2, tokens, D)
    embedded, early = xy_reduce(found, 0)
    level_hot = (levels[:, None] == jnp.arange(BINS)[None, :]).astype(F32)
    state = math.sqrt(D) * embedded.astype(F32) + jnp.dot(level_hot, value_table, precision=HIGHEST)

    if short:
        mats_all = jnp.stack(mats_all)
        gathers = []
        for group in range(2):
            part = [
                lax.dynamic_index_in_dim(mats_all, z ^ p, 0, False)
                for p in range(group * planes // 2, (group + 1) * planes // 2)
            ]
            gathers.append(PlaneGather(jnp.stack(part), x, y, c))
        gathers[0].one()
        gathers[0].two()
        gathers[1].one()
        mats = gathers[0].three(0, None)
    else:
        whole = lax.all_gather(mats_low, ("z", "x", "c", "y"), tiled=True).reshape(-1, D, D)
        mats = jnp.concatenate([whole, jnp.zeros((STORE - whole.shape[0], D, D), BF16)])

    queries, keys, values, near, store = begin(state, mats)
    stats = []
    for layer in range(LAYERS):
        far = flip(near, "c")
        if short and layer == 0:
            gathers[1].two()
        if short and layer == 1:
            mats = gathers[1].three(3 * LAYERS, mats)
        stat, *rest, store = layer_forward(
            state, queries, keys, values, far, places, vectors[layer], mats, store, layer
        )
        stats.append(stat)
        if layer < LAYERS - 1:
            state, queries, keys, values, near = rest

    pooled = (rest[0] + flip(rest[0], "c")) / counts[:, None]
    pooled = ordered(pooled, flip(pooled, "y"), y)
    pooled = ordered(pooled, flip(pooled, "x"), x)
    pooled_low = pooled.reshape(plane_cells, D).astype(BF16)
    loss_part, grad_pred, grad_pooled = call(
        partial(head_kernel, rows_dev, 2.0 / vocab, own_rows),
        [((8, 128), F32), ((plane_cells, col_rows), BF16), ((plane_cells, D), F32)],
        (pooled_low, table_col, target_col),
    )
    loss_part = loss_part[0, 0]
    grad_pooled = grad_pooled.reshape(2, 2, CELLS_ROW, D)
    grad_pooled = pick(grad_pooled, x) + flip(pick(grad_pooled, 1 - x), "x")
    grad_pooled = pick(grad_pooled, y) + flip(pick(grad_pooled, 1 - y), "y")
    gradient = grad_pooled / counts[:, None]

    parts = [None] * (6 * LAYERS)
    late = late_blocks = None
    vec_grads = [None] * LAYERS

    def gradients_of(low, high):
        rows = (8 * mat_rows * low, 8 * mat_rows * high)
        return PlaneReduce(*split_rows(parts, *rows, high - low, mat_rows, c), x, y)

    for layer in reversed(range(LAYERS)):
        span = slice(6 * layer, 6 * layer + 6)
        needed, more = (), lambda part: ()
        if short and layer == 1:

            def more(part):
                nonlocal late
                parts[9:12] = [(part, 1), (part, 2), (part, 3)]
                late = gradients_of(planes // 2, planes)
                return ()

        if short and layer == 0:
            late.one()
            needed = late.block
            more = lambda part: late.halves

        gradient, parts[span], vec_grads[layer] = layer_backward(
            gradient, stats[layer], store, places, vectors[layer], mats, layer, needed, more
        )

    grad_value = jnp.einsum("tb,td->bd", level_hot, gradient, precision=HIGHEST)
    grad_embedded = (math.sqrt(D) * gradient).astype(BF16)
    grad_plane, early = xy_gather(grad_embedded, 0)
    rest = gradients_of(0, planes // 2 if short else planes)
    rest.one()
    grad_col = dot_tn(hot, grad_plane.reshape(-1, D))
    grad_own = grad_col[:own_rows] + flip(grad_col[own_rows:].astype(BF16), "c").astype(F32)
    grad_own = grad_own + dot_tn(grad_pred[:, :own_rows], pooled_low)
    grad_own = grad_own.astype(BF16).reshape(planes, SLOT, D)[:, :rows_dev]
    if short:
        swaps = [z_swap(grad_own[k], k, planes) for k in range(1, planes)]
        grad_table = sum(term.astype(F32) for term in [grad_own[0], *swaps])
        blocks = jnp.concatenate([rest.two(grad_own), late.two(grad_own)])
        blocks = [lax.dynamic_index_in_dim(blocks, z ^ k, 0, False) for k in range(planes)]
        terms = [blocks[0]] + [z_swap(blocks[k], k, planes) for k in range(1, planes)]
        grad_matrices = sum(term.astype(F32) for term in terms)
    else:
        swaps = ()
        grad_table = jnp.sum(lax.all_to_all(grad_own, "z", 0, 0).astype(F32), axis=0)
        grad_matrices = owner_sum(rest.two(), 0, z, planes)

    small = jnp.concatenate([jnp.concatenate(vec_grads), grad_value])
    small = all_sum(small, planes)
    grad_vectors = small[: 6 * LAYERS].reshape(vectors.shape)
    grad_value = small[6 * LAYERS :]
    squares = jnp.sum(grad_matrices * grad_matrices) + jnp.sum(grad_table * grad_table)
    lanes = jnp.arange(128)[None, :]
    sums = jnp.where(lanes == 0, squares, jnp.where(lanes == 1, loss_part, 0.0))
    sums = small_sum(jnp.broadcast_to(sums, (8, 128)), x, y, z, planes)
    loss_sum = sums[0, 1]
    grad_norm = jnp.sqrt(sums[0, 0] + jnp.sum(small * small))
    factor = CLIP_NORM / grad_norm

    def update(weight, moment, average, grad_full):
        clipped = factor * grad_full
        moment_new = MOMENTUM * moment + clipped
        weight_new = weight - LEARN_RATE * (clipped + MOMENTUM * moment_new)
        return (
            moment_new,
            weight_new,
            AVERAGE_DECAY * average + (1.0 - AVERAGE_DECAY) * weight_new,
        )

    return (
        loss_sum,
        grad_norm,
        *update(matrices, matrices_mom, matrices_avg, grad_matrices),
        *update(vectors, vectors_mom, vectors_avg, grad_vectors),
        *update(value_table, value_mom, value_avg, grad_value),
        *update(gene_table, gene_mom, gene_avg, grad_table),
    )


def solution(mesh):
    devices = mesh.devices
    fine = Mesh(devices.reshape(devices.shape[0] // 4, 2, 2, devices.shape[1]), ("z", "x", "c", "y"))
    dp = ("z", "x", "c")
    every = ("z", "x", "c", "y")
    weights = (P(every, None), P(), P(), P(every, None))
    in_specs = (P(dp, None),) * 3 + (P(dp, None, None), P(None, every)) + weights * 3
    out_specs = (P(), P()) + (P(every, None),) * 3 + (P(),) * 6 + (P(every, None),) * 3
    return jax.shard_map(local, mesh=fine, in_specs=in_specs, out_specs=out_specs, check_vma=False)
```

```python
from functools import partial
import itertools
import math

import jax
import jax.numpy as jnp
from jax import lax
from jax.experimental import pallas as pl
from jax.experimental.pallas import tpu as pltpu
from jax.sharding import Mesh, PartitionSpec as P

D = 512
HEADS = 8
HEAD_DIM = 64
BINS = 51
LAYERS = 3
CELLS_ROW = 4
PAIR = 128
SLOT = 256

EPSILON = 1e-05
NEGATIVE = -1e30
LEARN_RATE = 200.0
MOMENTUM = 0.9
AVERAGE_DECAY = 0.7
CLIP_NORM = 0.25
HIGHEST = lax.Precision.HIGHEST
SCALING = 1.0 / math.sqrt(HEAD_DIM)
F32 = jnp.float32
BF16 = jnp.bfloat16


def flip(block, axis):
    return lax.ppermute(block, axis, [(0, 1), (1, 0)])


def after(values, *needed):
    values, tree = jax.tree.flatten(values)
    needed = jax.tree.leaves(needed)
    if not needed:
        return tree.unflatten(values)
    anywhere = pl.BlockSpec(memory_space=pl.ANY)
    values = pl.pallas_call(
        lambda *refs: None,
        out_shape=[jax.ShapeDtypeStruct(v.shape, v.dtype) for v in values],
        in_specs=[anywhere] * (len(values) + len(needed)),
        out_specs=[anywhere] * len(values),
        input_output_aliases={i: i for i in range(len(values))},
    )(*values, *needed)
    return tree.unflatten(values)


def ordered(own, other, bit, axis=0):
    low = jnp.where(bit == 0, own, other)
    high = jnp.where(bit == 0, other, own)
    return jnp.stack([low, high], axis=axis)


def pick(pair, bit, axis=0):
    first = lax.index_in_dim(pair, 0, axis, False)
    second = lax.index_in_dim(pair, 1, axis, False)
    return jnp.where(bit == 0, first, second)


def short_z(planes):
    return planes == 4


def slot_of(plane, z, planes):
    return plane ^ z if short_z(planes) else plane


def z_swap(block, k, planes, targets=None):
    pairs = [(p ^ k, p) for p in range(planes) if targets is None or p in targets]
    return lax.ppermute(block, "z", pairs)


def xy_gather(block, cut_axis):
    first, second = jnp.split(block, 2, axis=cut_axis)
    early = (flip(first, "x"), flip(second, "y"))
    first = jnp.stack([first, early[0]])
    second = jnp.stack([second, early[1]])
    first = jnp.stack([first, flip(first, "y")], axis=1)
    second = jnp.stack([second, flip(second, "x")], axis=0)
    return (jnp.concatenate([first, second], axis=cut_axis + 2), early)


def rounded_sum(a, b):
    return (a.astype(F32) + b.astype(F32)).astype(a.dtype)


def xy_reduce(blocks, cut_axis):
    first, second = jnp.split(blocks, 2, axis=cut_axis + 2)
    early = (flip(first[1], "x"), flip(second[:, 1], "y"))
    first = rounded_sum(first[0], early[0])
    second = rounded_sum(second[:, 0], early[1])
    first = rounded_sum(first[0], flip(first[1], "y"))
    second = rounded_sum(second[0], flip(second[1], "x"))
    return (jnp.concatenate([first, second], axis=cut_axis), early)


def by_distance(blocks, bit, axis):
    return jnp.where(bit == 0, blocks, jnp.flip(blocks, axis))


class PlaneGather:
    def __init__(self, block, x, y, c):
        self.block, self.bits = block, (x, y, c)

    def one(self, *needed):
        first, second = after(tuple(jnp.split(self.block, 2, axis=1)), *needed)
        self.early = (flip(first, "x"), flip(second, "y"))
        self.halves = (
            ordered(first, self.early[0], self.bits[0], 1),
            ordered(second, self.early[1], self.bits[1], 1),
        )

    def two(self, *needed):
        first, second = after(self.halves, *needed)
        first = ordered(first, flip(first, "y"), self.bits[1], 2)
        second = ordered(second, flip(second, "x"), self.bits[0], 1)
        self.block = jnp.concatenate([first, second], axis=3)

    def three(self, base, store, *needed):
        block = after(self.block, *needed)
        count = 2 * block.size // (D * D)
        return call(
            partial(join_kernel, base), [], (block, flip(block, "c")), [pltpu.VMEM((D, D), BF16)] * count,
            scalars=(self.bits[2][None],), store=store, fresh=store is None,
        )[-1]


class PlaneReduce:
    def __init__(self, near, far, x, y):
        self.bits = (x, y)
        self.block = rounded_sum(near, flip(far, "c"))

    def one(self, *needed):
        x, y = self.bits
        first, second = jnp.split(self.block, 2, axis=3)
        far = after((pick(first, 1 - x, 1), pick(second, 1 - y, 2)), *needed)
        first = rounded_sum(pick(first, x, 1), flip(far[0], "x"))
        second = rounded_sum(pick(second, y, 2), flip(far[1], "y"))
        self.halves = (first, second)

    def two(self, *needed):
        x, y = self.bits
        first, second = self.halves
        far = after((pick(first, 1 - y, 1), pick(second, 1 - x, 1)), *needed)
        first = rounded_sum(pick(first, y, 1), flip(far[0], "y"))
        second = rounded_sum(pick(second, x, 1), flip(far[1], "x"))
        return jnp.concatenate([first, second], axis=1)


def owner_sum(blocks, group, z, planes):
    if not short_z(planes):
        return jnp.sum(lax.all_to_all(blocks, "z", 0, 0).astype(F32), axis=0)
    odd = z & 1
    held = pick(blocks, odd).astype(F32) + z_swap(pick(blocks, 1 - odd), 1, planes).astype(F32)
    got = z_swap(held.astype(BF16), 2, planes, (2 * group, 2 * group + 1))
    return jnp.where(z >> 1 == group, held, 0.0) + got.astype(F32)


def small_sum(block, x, y, z, planes):
    block = block + flip(block, "c")
    near = [block] + [
        lax.ppermute(block, ("x", "y"), [(i, i ^ k) for i in range(4)]) for k in range(1, 4)
    ]
    near = jnp.stack(near)
    at = lambda stack, i: lax.dynamic_index_in_dim(stack, i, 0, False)
    place = 2 * x + y
    block = sum(at(near, place ^ i) for i in range(4))
    if not short_z(planes):
        return lax.psum(block, "z")
    far = jnp.stack([block] + [z_swap(block, k, planes) for k in range(1, planes)])
    return sum(at(far, z ^ i) for i in range(planes))


def all_sum(block, planes):
    for axis in ("c", "x", "y"):
        block = block + flip(block, axis)
    if not short_z(planes):
        return lax.psum(block, "z")
    k = 1
    while k < planes:
        block = block + z_swap(block, k, planes)
        k *= 2
    return block


LIMIT = 40 * 2**20
COST = 10**9
STORE = 132


class Moves:
    def __init__(self, sources, buffers, fetch_sems, store, save_sems):
        self.copies = [
            pltpu.make_async_copy(source, buffer, fetch_sems.at[i])
            for i, (source, buffer) in enumerate(zip(sources, buffers))
        ]
        for copy in self.copies:
            copy.start()
        self.buffers, self.waiting = buffers, set(range(len(buffers)))
        self.store, self.sems, self.saves = store, save_sems, []

    def get(self, i):
        if i in self.waiting:
            self.copies[i].wait()
            self.waiting.remove(i)
        return self.buffers[i]

    def put(self, square, ref, rows=None):
        target = self.store.at[square]
        if rows is not None:
            target = target.at[rows]
        copy = pltpu.make_async_copy(ref, target, self.sems.at[len(self.saves)])
        copy.start()
        self.saves.append(copy)

    def finish(self):
        for i in sorted(self.waiting):
            self.copies[i].wait()
        for copy in self.saves:
            copy.wait()


def call(body, outs, args, scratch=(), needed=(), scalars=(), fetch=(), store=None, fresh=False):
    needed = jax.tree.leaves(needed)
    saving = fresh or store is not None
    shapes = [jax.ShapeDtypeStruct(*o) for o in outs]
    if saving:
        shapes.append(jax.ShapeDtypeStruct((STORE, D, D), BF16))
    olds = [] if store is None else [store]
    counts = [len(scalars) + len(args), len(fetch), len(needed) + len(olds), len(outs), int(saving)]
    counts += [len(fetch), len(scratch)]

    def kernel(*refs):
        groups, at = [], 0
        for count in counts:
            groups.append(refs[at : at + count])
            at += count
        ins, sources, _, results, target, buffers, spare = groups
        sources = [ref.at[square] for ref, (_, square) in zip(sources, fetch)]
        moves = Moves(sources, buffers, refs[at], target[0] if saving else None, refs[at + 1])
        extra = (moves,) if saving or fetch else ()
        body(*extra, *ins, *results, *spare)
        moves.finish()

    small, anywhere = pl.BlockSpec(memory_space=pltpu.SMEM), pl.BlockSpec(memory_space=pl.ANY)
    near = pl.BlockSpec(memory_space=pltpu.VMEM)
    first = len(scalars) + len(args) + len(fetch) + len(needed)
    return pl.pallas_call(
        kernel,
        out_shape=shapes,
        in_specs=[small] * len(scalars)
        + [near] * len(args)
        + [anywhere] * (len(fetch) + len(needed) + len(olds)),
        out_specs=[near] * len(outs) + [anywhere] * int(saving),
        input_output_aliases={first: len(outs)} if olds else {},
        scratch_shapes=[pltpu.VMEM((D, D), BF16)] * len(fetch)
        + list(scratch)
        + [pltpu.SemaphoreType.DMA((max(1, len(fetch)),)), pltpu.SemaphoreType.DMA((24,))],
        compiler_params=pltpu.CompilerParams(vmem_limit_bytes=LIMIT),
        cost_estimate=pl.CostEstimate(flops=COST, bytes_accessed=COST // 1000, transcendentals=0),
    )(*scalars, *args, *(a for a, _ in fetch), *needed, *olds)


def dot(a, b):
    return jnp.dot(a, b, preferred_element_type=F32)


def dot_tn(a, b):
    return lax.dot_general(a, b, (((0,), (0,)), ((), ())), preferred_element_type=F32)


def dot_nt(a, b):
    return lax.dot_general(a, b, (((1,), (1,)), ((), ())), preferred_element_type=F32)


def head_marks(width):
    rows = lax.broadcasted_iota(jnp.int32, (D, width), 0) // HEAD_DIM
    return (rows == lax.broadcasted_iota(jnp.int32, (D, width), 1)).astype(F32)


def lane_marks(side, value):
    lanes = lax.broadcasted_iota(jnp.int32, (1, PAIR), 1) // HEAD_DIM
    return jnp.where(lanes == side, value, 0.0)


def norm(summed):
    average = jnp.mean(summed, axis=-1, keepdims=True)
    centered = summed - average
    scaling = lax.rsqrt(jnp.mean(centered * centered, axis=-1, keepdims=True) + EPSILON)
    return (centered * scaling, scaling)


def norm_pull(weighted, normed, scaling):
    centered = weighted - jnp.mean(weighted, axis=-1, keepdims=True)
    return scaling * (centered - normed * jnp.mean(weighted * normed, axis=-1, keepdims=True))


def project(low, rows, moves, first, q_ref, k_ref, v_ref, near_ref):
    quarter = near_ref.shape[0]
    keys = dot(low, moves.get(first + 1)[...]).astype(BF16)
    values = dot(low, moves.get(first + 2)[...]).astype(BF16)
    k_ref[rows] = keys
    v_ref[rows] = values
    if rows.start == 0:
        near_ref[:, :D] = keys[:quarter]
        near_ref[:, D:] = values[:quarter]
    q_ref[rows] = dot(low, moves.get(first)[...]).astype(BF16)


def first_kernel(moves, x_ref, q_ref, k_ref, v_ref, near_ref, low_ref):
    low = x_ref[...].astype(BF16)
    low_ref[...] = low
    moves.put(LOW, low_ref)
    rows = slice(0, x_ref.shape[0])
    project(low, rows, moves, 0, q_ref, k_ref, v_ref, near_ref)
    for i, ref in enumerate((q_ref, k_ref, v_ref)):
        moves.put(LOW + 1 + i, ref)


def weigh(marks, array):
    return lax.dot_general(
        marks, array, (((0,), (1,)), ((), ())), preferred_element_type=F32, precision=HIGHEST
    )[:HEADS]


def spread(marks, array):
    return lax.dot_general(
        array.astype(BF16), marks[:, :HEADS].astype(BF16), (((0,), (1,)), ((), ())),
        preferred_element_type=F32,
    )


def forward_kernel(last, base, moves, *refs):
    x_ref, q_ref, k_ref, v_ref, far_ref, own_row_ref, key_col_ref, own_col_ref, vec_ref = refs[:9]
    outs, refs = (refs[9:11], refs[11:]) if last else (refs[9:15], refs[15:])
    stat_ref, outs = outs[0], outs[1:]
    mix_ref, u1_ref, low1_ref, slope_ref, act_ref, u2_ref, low_ref = refs[:7]
    keys_ref, values_ref, bias_ref, own_ref, wide_ref, turned_ref, scale_ref, prob_ref = refs[7:]
    moves.put(base + FAR, far_ref.at[:, :D], slice(0, far_ref.shape[0]))
    moves.put(base + FAR, far_ref.at[:, D:], slice(far_ref.shape[0], x_ref.shape[0]))
    tokens = x_ref.shape[0]
    quarter = far_ref.shape[0]
    far_half = slice(quarter, tokens)
    keys_ref[:quarter] = k_ref[:quarter]
    keys_ref[quarter:] = far_ref[:, :D]
    values_ref[:, :quarter] = v_ref[:quarter].T
    values_ref[:, quarter:] = far_ref[:, D:].T
    bias_ref[...] = jnp.where(key_col_ref[...] == own_row_ref[...], 0.0, NEGATIVE)
    marks = head_marks(PAIR)
    product = q_ref[far_half].astype(F32) * k_ref[far_half].astype(F32) * SCALING
    own_ref[...] = weigh(marks, product)

    def pair_step(pair, carry):
        lanes = slice(pair * PAIR, pair * PAIR + PAIR)
        key_pair = keys_ref[:, lanes]
        q_pair = q_ref[:, lanes]
        for side in range(2):
            head = slice(2 * pair + side, 2 * pair + side + 1)
            scaled = q_pair * lane_marks(side, SCALING).astype(BF16)
            for start in range(0, tokens, 256):
                spots = slice(start, start + 256)
                scores = dot_nt(key_pair, scaled[spots]) + bias_ref[:, spots]
                top = jnp.max(scores, axis=0, keepdims=True)
                if start >= quarter:
                    far_spots = slice(start - quarter, start - quarter + 256)
                    own = own_ref[head, far_spots]
                    top = jnp.maximum(top, own)
                exps = jnp.exp(scores - top)
                amount = jnp.sum(exps, axis=0, keepdims=True)
                if start >= quarter:
                    own = jnp.exp(own - top)
                    amount = amount + own
                inverse = 1.0 / amount
                if start >= quarter:
                    own_ref[head, far_spots] = own * inverse
                stat_ref[head, spots] = top + jnp.log(amount)
                prob_ref[:, spots] = (exps * inverse).astype(BF16)
            part = slice(pair * PAIR + side * HEAD_DIM, pair * PAIR + side * HEAD_DIM + HEAD_DIM)
            turned_ref[part, :] = dot(values_ref[part, :], prob_ref[...])
        return carry

    for pair in range(D // PAIR):
        pair_step(pair, 0)
    wide_ref[...] = turned_ref[...].T
    own_share = spread(marks, own_ref[...]) * v_ref[far_half].astype(F32)
    mix_ref[:quarter] = wide_ref[:quarter].astype(BF16)
    mix_ref[far_half] = (wide_ref[far_half] + own_share).astype(BF16)
    moves.put(base + MIX, mix_ref)
    sums = [jnp.zeros((1, D), F32) for _ in range(CELLS_ROW)]
    for start in range(0, tokens, tokens):
        rows = slice(start, start + tokens)
        normed, scaling = norm(x_ref[rows] + dot(mix_ref[rows], moves.get(0)[...]))
        u1_ref[rows] = normed.astype(BF16)
        scale_ref[rows, 0:1] = scaling
        first = normed * vec_ref[0:1] + vec_ref[1:2]
        first_low = first.astype(BF16)
        low1_ref[rows] = first_low
        hidden = dot(first_low, moves.get(1)[...]) + vec_ref[4:5]
        share = 0.5 + 0.5 * lax.erf(hidden * math.sqrt(0.5))
        active = (hidden * share).astype(BF16)
        act_ref[rows] = active
        density = jnp.exp(-0.5 * hidden * hidden) * (1.0 / math.sqrt(2.0 * math.pi))
        slope_ref[rows] = (share + hidden * density).astype(BF16)
        normed, scaling = norm(first + dot(active, moves.get(2)[...]) + vec_ref[5:6])
        u2_ref[rows] = normed.astype(BF16)
        scale_ref[rows, 1:2] = scaling
        state = normed * vec_ref[2:3] + vec_ref[3:4]
        for i, ref in enumerate((u1_ref, low1_ref, slope_ref, act_ref, u2_ref)):
            moves.put(base + U1 + i, ref.at[rows], rows)
        if last:
            for cell in range(CELLS_ROW):
                part = jnp.where(own_col_ref[rows] == cell, state, 0.0)
                sums[cell] = sums[cell] + jnp.sum(part, axis=0, keepdims=True)
        else:
            outs[0][rows] = state
            low = state.astype(BF16)
            low_ref[rows] = low
            project(low, rows, moves, 3, *outs[1:])
    stat_ref[HEADS:] = scale_ref[...].T[:HEADS]
    if last:
        outs[0][...] = jnp.concatenate(sums)
    else:
        for i, ref in enumerate((low_ref, *outs[1:4])):
            moves.put(base + NEXT + i, ref)


def head_kernel(rows_dev, scale, own_rows, pooled_ref, table_ref, target_ref, loss_ref, low_ref, grad_ref):
    table = table_ref[...]
    errors = dot_nt(pooled_ref[...], table) - (target_ref[...] * (4.0 / (BINS - 1)) - 2.0)
    spot = lax.broadcasted_iota(jnp.int32, errors.shape, 1) % SLOT
    errors = jnp.where(spot < rows_dev, errors, 0.0)
    mine = errors[:, :own_rows]
    loss_ref[...] = jnp.broadcast_to(jnp.sum(mine * mine), loss_ref.shape)
    low = (errors * scale).astype(BF16)
    low_ref[...] = low
    grad_ref[...] = dot(low, table)


def backward_kernel(
    seeded, moves,
    grad_ref, own_col_ref, stat_ref, own_row_ref, key_col_ref, vec_ref,
    sum1_ref, low2_ref, hid_ref, low1_ref, gq_ref, gk_ref, gv_ref, send_ref, gvec_ref,
    keys_ref, values_ref, bias_ref, gmix_ref, own_p_ref, own_s_ref, turned_ref, wide_ref, scale_ref,
    score_ref, prob_ref,
):
    bias_ref[...] = jnp.where(key_col_ref[...] == own_row_ref[...], 0.0, NEGATIVE)
    scale_ref[...] = stat_ref[HEADS:].T
    u2_ref, w2_ref, slope_ref, w1_ref = (moves.get(i) for i in range(4))
    q_ref = moves.buffers[6]
    lse_ref = stat_ref
    tokens = q_ref.shape[0]
    quarter = tokens // 2
    sums = [jnp.zeros((1, D), F32) for _ in range(6)]

    def gather(index, value):
        sums[index] = sums[index] + jnp.sum(value, axis=0, keepdims=True)

    for start in range(0, tokens, quarter):
        rows = slice(start, start + quarter)
        if seeded:
            upstream = jnp.zeros((quarter, D), F32)
            for cell in range(CELLS_ROW):
                upstream = jnp.where(own_col_ref[rows] == cell, grad_ref[cell : cell + 1], upstream)
        else:
            upstream = grad_ref[rows]
        normed = u2_ref[rows].astype(F32)
        gather(2, upstream * normed)
        gather(3, upstream)
        sum_two = norm_pull(upstream * vec_ref[2:3], normed, scale_ref[rows, 1:2])
        low_two = sum_two.astype(BF16)
        low2_ref[rows] = low_two
        gather(5, low_two.astype(F32))
        hid = (dot_nt(low_two, w2_ref[...]) * slope_ref[rows].astype(F32)).astype(BF16)
        hid_ref[rows] = hid
        gather(4, hid.astype(F32))
        upstream = sum_two + dot_nt(hid, w1_ref[...])
        normed = moves.get(4)[rows].astype(F32)
        gather(0, upstream * normed)
        gather(1, upstream)
        sum_one = norm_pull(upstream * vec_ref[0:1], normed, scale_ref[rows, 0:1])
        sum1_ref[rows] = sum_one
        low_one = sum_one.astype(BF16)
        low1_ref[rows] = low_one
        gmix_ref[rows] = dot_nt(low_one, moves.get(5)[...]).astype(BF16)
    gvec_ref[...] = jnp.concatenate(sums + [jnp.zeros((2, D), F32)])

    q_ref, k_ref, v_ref, far_ref = (moves.get(i) for i in range(6, 10))
    keys_ref[:quarter] = k_ref[:quarter]
    keys_ref[quarter:] = far_ref[:quarter]
    values_ref[:quarter] = v_ref[:quarter]
    values_ref[quarter:] = far_ref[quarter:]
    turned_ref[...] = keys_ref[...].T
    marks = head_marks(PAIR)
    far_half = slice(quarter, tokens)
    queries = q_ref[far_half].astype(F32)
    mixed = gmix_ref[far_half].astype(F32)
    product = queries * k_ref[far_half].astype(F32) * SCALING
    own_prob = jnp.exp(weigh(marks, product) - lse_ref[:HEADS, far_half])
    own_grad = weigh(marks, mixed * v_ref[far_half].astype(F32))
    own_p_ref[...] = own_prob
    own_s_ref[...] = own_grad

    def pair_step(pair, carry):
        lanes = slice(pair * PAIR, pair * PAIR + PAIR)
        key_pair = keys_ref[:, lanes]
        value_pair = values_ref[:, lanes]
        q_pair = q_ref[:, lanes]
        mix_pair = gmix_ref[:, lanes]
        grad_k = jnp.zeros((tokens, PAIR), F32)
        grad_v = jnp.zeros((tokens, PAIR), F32)
        for side in range(2):
            head = 2 * pair + side
            scaled = q_pair * lane_marks(side, SCALING).astype(BF16)
            mix_side = mix_pair * lane_marks(side, 1.0).astype(BF16)
            for start in range(0, tokens, 256):
                spots = slice(start, start + 256)
                prob = dot_nt(key_pair, scaled[spots]) + bias_ref[:, spots]
                prob = jnp.exp(prob - lse_ref[slice(head, head + 1), spots])
                grad_p = dot_nt(value_pair, mix_side[spots])
                delta = jnp.sum(prob * grad_p, axis=0, keepdims=True)
                if start >= quarter:
                    far_spots = slice(start - quarter, start - quarter + 256)
                    own_p = own_p_ref[slice(head, head + 1), far_spots]
                    own_g = own_s_ref[slice(head, head + 1), far_spots]
                    delta = delta + own_p * own_g
                    own_s_ref[slice(head, head + 1), far_spots] = own_p * (own_g - delta)
                score_ref[:, spots] = (prob * (grad_p - delta)).astype(BF16)
                prob_ref[:, spots] = prob.astype(BF16)
            grad_s = score_ref[...]
            grad_k = grad_k + dot(grad_s, scaled)
            grad_v = grad_v + dot(prob_ref[...], mix_side)
            part = slice(pair * PAIR + side * HEAD_DIM, pair * PAIR + side * HEAD_DIM + HEAD_DIM)
            wide_ref[part, :] = dot(turned_ref[part, :], grad_s)
        gk_ref[:, lanes] = grad_k
        gv_ref[:, lanes] = grad_v
        return carry

    for pair in range(D // PAIR):
        pair_step(pair, 0)
    send_ref[:, :D] = gk_ref[quarter:].astype(BF16)
    send_ref[:, D:] = gv_ref[quarter:].astype(BF16)
    own_score = spread(marks, own_s_ref[...]) * SCALING
    gv_ref[far_half] = spread(marks, own_p_ref[...]) * mixed
    gk_ref[far_half] = own_score * queries
    grad_q = wide_ref[...].T * SCALING
    gq_ref[:quarter] = grad_q[:quarter].astype(BF16)
    gq_ref[far_half] = (grad_q[far_half] + own_score * k_ref[far_half].astype(F32)).astype(BF16)


def weights_kernel(moves, gq_ref, g1_ref, gz_ref, g2_ref, out_ref):
    for i, ref in enumerate((gq_ref, g1_ref, gz_ref, g2_ref)):
        out_ref[i] = dot_tn(moves.get(i)[...], ref[...]).astype(BF16)


def inputs_kernel(
    moves, sum1_ref, gq_ref, gk_ref, gv_ref, got_ref, grad_ref, out_ref, low_k_ref, low_v_ref
):
    quarter = got_ref.shape[0]
    low_k_ref[:quarter] = (gk_ref[:quarter] + got_ref[:, :D].astype(F32)).astype(BF16)
    low_v_ref[:quarter] = (gv_ref[:quarter] + got_ref[:, D:].astype(F32)).astype(BF16)
    low_k_ref[quarter:] = gk_ref[quarter:].astype(BF16)
    low_v_ref[quarter:] = gv_ref[quarter:].astype(BF16)
    grad_ref[...] = (
        sum1_ref[...]
        + dot_nt(gq_ref[...], moves.get(0)[...])
        + dot_nt(low_k_ref[...], moves.get(1)[...])
        + dot_nt(low_v_ref[...], moves.get(2)[...])
    )
    low = moves.get(3)[...]
    out_ref[0] = dot_tn(low, low_k_ref[...]).astype(BF16)
    out_ref[1] = dot_tn(low, low_v_ref[...]).astype(BF16)


def join_kernel(base, moves, c_ref, own_ref, got_ref, *outs):
    count, _, _, rows, _ = own_ref.shape
    mine = c_ref[0] == 0
    for i, (plane, x, c, y) in enumerate(itertools.product(range(count), (0, 1), (0, 1), (0, 1))):
        at, end = rows * i, rows * (i + 1)
        while at < end:
            place, stop = at // D, min(end, (at // D + 1) * D)
            piece = slice(at - rows * i, stop - rows * i)
            own, got = own_ref[plane, x, y, piece], got_ref[plane, x, y, piece]
            chosen = jnp.where(mine, own, got) if c == 0 else jnp.where(mine, got, own)
            outs[place][at - place * D : stop - place * D] = chosen
            at = stop
            if at == place * D + D:
                moves.put(base + place, outs[place])


def split_kernel(plan, c_ref, *refs):
    ins, (near_ref, far_ref) = refs[:-2], refs[-2:]
    count, _, _, rows, _ = near_ref.shape
    mine = c_ref[0] == 0
    at = 0
    for place, index, low, size in plan:
        done = 0
        while done < size:
            i = at // rows
            step = min(size - done, rows * (i + 1) - at)
            plane, x, c, y = i // 8, i // 4 % 2, i // 2 % 2, i % 2
            piece = slice(at - rows * i, at - rows * i + step)
            value = ins[place][index, low + done : low + done + step]
            stays = mine if c == 0 else jnp.logical_not(mine)

            @pl.when(stays)
            def _():
                near_ref[plane, x, y, piece] = value

            @pl.when(jnp.logical_not(stays))
            def _():
                far_ref[plane, x, y, piece] = value

            at, done = at + step, done + step


def shapes_of(tokens):
    return (((tokens, D), F32), ((tokens, D), BF16), ((tokens // 2, 2 * D), BF16))


def vmem(*shape_types):
    return [pltpu.VMEM(*s) for s in shape_types]


SQUARES = 16
LOW, NEXT, FAR, MIX, U1 = 0, 16, 4, 5, 6


def begin(state, mats):
    wide, slim, half = shapes_of(state.shape[0])
    fetch = [(mats, i) for i in range(3)]
    return call(first_kernel, [slim, slim, slim, half], (state,), vmem(slim), fetch=fetch, fresh=True)


def layer_forward(state, queries, keys, values, far, places, vecs, mats, store, layer):
    tokens = state.shape[0]
    wide, slim, half = shapes_of(tokens)
    last = layer == LAYERS - 1
    square = ((tokens, tokens), F32)
    own, turned = ((HEADS, tokens // 2), F32), ((D, tokens), F32)
    outs = [((2 * HEADS, tokens), F32)]
    outs += [((CELLS_ROW, D), F32)] if last else [wide, slim, slim, slim, half]
    own_col, own_row, key_col = places
    return call(
        partial(forward_kernel, last, SQUARES * layer),
        outs,
        (state, queries, keys, values, far, own_row, key_col, own_col, vecs),
        vmem(*[slim] * 7, slim, ((D, tokens), BF16), square, own, wide, turned, ((tokens, PAIR), F32),
            ((tokens, tokens), BF16)),
        fetch=[(mats, 6 * layer + i) for i in range(3, 6 if last else 9)],
        store=store,
    )


def layer_backward(gradient, stat, store, places, vecs, mats, layer, needed, more):
    tokens = stat.shape[1]
    wide, slim, half = shapes_of(tokens)
    own_col, own_row, key_col = places
    own, square = ((HEADS, tokens // 2), F32), ((tokens, tokens), F32)
    at, mat = SQUARES * layer, 6 * layer
    saved = lambda *squares: [(store, at + i) for i in squares]
    sum1, g2, gz, g1, gq, gk, gv, send, gvec = call(
        partial(backward_kernel, gradient.shape[0] == CELLS_ROW),
        [wide, slim, slim, slim, slim, wide, wide, half, ((8, D), F32)],
        (gradient, own_col, stat, own_row, key_col, vecs),
        vmem(
            slim, slim, square, slim, own, own, ((D, tokens), BF16), ((D, tokens), F32),
            ((tokens, HEADS), F32), ((tokens, tokens), BF16), ((tokens, tokens), BF16),
        ),
        needed,
        fetch=[
            *saved(U1 + 4), (mats, mat + 5), *saved(U1 + 2), (mats, mat + 4), *saved(U1),
            (mats, mat + 3), *saved(LOW + 1, LOW + 2, LOW + 3, FAR),
        ],
    )
    (part_one,) = call(
        weights_kernel,
        [((4, D, D), BF16)],
        (gq, g1, gz, g2),
        fetch=saved(LOW, MIX, U1 + 1, U1 + 3),
    )
    grad, part_two = call(
        inputs_kernel,
        [wide, ((2, D, D), BF16)],
        (sum1, gq, gk, gv, flip(send, "c")),
        vmem(slim, slim),
        more(part_one),
        fetch=[*((mats, mat + i) for i in range(3)), *saved(LOW)],
    )
    parts = [(part_one, 0), (part_two, 0), (part_two, 1), (part_one, 1), (part_one, 2), (part_one, 3)]
    return (grad, parts, gvec[:6])


def split_rows(parts, low, high, count, rows, c):
    arrays, plan = [], []
    for i in range(low // D, -(-high // D)):
        array, index = parts[i]
        known = [j for j, a in enumerate(arrays) if a is array]
        if not known:
            arrays.append(array)
            known = [len(arrays) - 1]
        start, stop = max(low, i * D), min(high, i * D + D)
        plan.append((known[0], index, start - i * D, stop - start))
    half = ((count, 2, 2, rows, D), BF16)
    return call(partial(split_kernel, plan), [half, half], arrays, scalars=(c[None],))


def local(
    gene_ids, expr_bins, gene_order, cell_ids, target_bins,
    matrices, vectors, value_table, gene_table,
    matrices_mom, vectors_mom, value_mom, gene_mom,
    matrices_avg, vectors_avg, value_avg, gene_avg,
):
    planes = lax.axis_size("z")
    short = short_z(planes)
    z, x, c, y = (lax.axis_index(a) for a in ("z", "x", "c", "y"))
    half = cell_ids.shape[2]
    quarter = half // 2
    rows_dev = gene_table.shape[0]
    vocab = rows_dev * planes * 8
    mat_rows = matrices.shape[0]
    plane_cells = 4 * CELLS_ROW

    mats_low = matrices.astype(BF16)
    if short:
        mats_all = [mats_low] + [z_swap(mats_low, k, planes) for k in range(1, planes)]

    codes = gene_ids[0] * 64 + expr_bins[0]
    mine = jnp.stack([codes, gene_order[0], cell_ids[0].reshape(-1)])
    mine = jnp.where(c == y, mine, flip(mine, "c"))
    codes, order, cells = mine[0], mine[1], mine[2]

    def own_part(array):
        return jnp.concatenate(
            [
                lax.dynamic_slice_in_dim(array, c * quarter, quarter),
                lax.dynamic_slice_in_dim(array, half + c * quarter, quarter),
            ]
        )

    picks = own_part(order)
    own_cells = own_part(cells)
    far_known = lax.dynamic_slice_in_dim(cells, (1 - c) * quarter, quarter)
    key_cells = jnp.concatenate([own_cells[:quarter], far_known])
    tokens = picks.shape[0]
    place = jnp.arange(codes.shape[0])
    code = jnp.sum(jnp.where(picks[:, None] == place[None, :], codes[None, :], 0), axis=1)
    genes, levels = code >> 6, code & 63
    places = (own_cells[:, None], own_cells[None, :], key_cells[:, None])
    numbers = jnp.arange(CELLS_ROW)
    counts = jnp.sum((cells[None, :] == numbers[:, None]).astype(F32), axis=1)

    plane_genes = xy_gather(genes, 0)[0].reshape(-1)

    table_low = gene_table.astype(BF16)
    targets = target_bins.astype(BF16).reshape(planes, plane_cells, rows_dev)
    targets = jnp.pad(targets, ((0, 0), (0, 0), (0, D - rows_dev)))
    if short:
        load = lambda k: jnp.concatenate(
            [table_low, lax.dynamic_index_in_dim(targets, z ^ k, 0, False)]
        )
        got = [load(0)] + [z_swap(load(k), k, planes) for k in range(1, planes)]
        slots = jnp.stack(got)
    else:
        rows = lax.all_gather(table_low, "z")
        slots = jnp.concatenate([rows, lax.all_to_all(targets, "z", 0, 0)], axis=1)
        got = [slots]
    table_col = jnp.stack([slots, flip(slots, "c")])
    target_col = table_col[:, :, rows_dev:, :SLOT].transpose(2, 0, 1, 3)
    table_col = table_col.reshape(-1, D)
    col_rows = table_col.shape[0]
    own_rows = col_rows // 2
    target_col = target_col.reshape(plane_cells, col_rows).astype(F32)

    owner, inner = plane_genes // rows_dev, plane_genes % rows_dev
    here = ((owner >> 2) & 1) * 2 + (owner & 1) == x * 2 + y
    slot = ((owner >> 1) & 1 ^ c) * planes + slot_of(owner >> 3, z, planes)
    index = jnp.where(here, slot * SLOT + inner, -1)
    hot = (index[:, None] == jnp.arange(col_rows)[None, :]).astype(BF16)
    found = dot(hot, table_col).astype(BF16).reshape(2, 2, tokens, D)
    embedded, early = xy_reduce(found, 0)
    level_hot = (levels[:, None] == jnp.arange(BINS)[None, :]).astype(F32)
    state = math.sqrt(D) * embedded.astype(F32) + jnp.dot(level_hot, value_table, precision=HIGHEST)

    if short:
        mats_all = jnp.stack(mats_all)
        gathers = []
        for group in range(2):
            part = [
                lax.dynamic_index_in_dim(mats_all, z ^ p, 0, False)
                for p in range(group * planes // 2, (group + 1) * planes // 2)
            ]
            gathers.append(PlaneGather(jnp.stack(part), x, y, c))
        gathers[0].one()
        gathers[0].two()
        gathers[1].one()
        mats = gathers[0].three(0, None)
    else:
        whole = lax.all_gather(mats_low, ("z", "x", "c", "y"), tiled=True).reshape(-1, D, D)
        mats = jnp.concatenate([whole, jnp.zeros((STORE - whole.shape[0], D, D), BF16)])

    queries, keys, values, near, store = begin(state, mats)
    stats = []
    for layer in range(LAYERS):
        far = flip(near, "c")
        if short and layer == 0:
            gathers[1].two()
        if short and layer == 1:
            mats = gathers[1].three(3 * LAYERS, mats)
        stat, *rest, store = layer_forward(
            state, queries, keys, values, far, places, vectors[layer], mats, store, layer
        )
        stats.append(stat)
        if layer < LAYERS - 1:
            state, queries, keys, values, near = rest

    pooled = (rest[0] + flip(rest[0], "c")) / counts[:, None]
    pooled = ordered(pooled, flip(pooled, "y"), y)
    pooled = ordered(pooled, flip(pooled, "x"), x)
    pooled_low = pooled.reshape(plane_cells, D).astype(BF16)
    loss_part, grad_pred, grad_pooled = call(
        partial(head_kernel, rows_dev, 2.0 / vocab, own_rows),
        [((8, 128), F32), ((plane_cells, col_rows), BF16), ((plane_cells, D), F32)],
        (pooled_low, table_col, target_col),
    )
    loss_part = loss_part[0, 0]
    grad_pooled = grad_pooled.reshape(2, 2, CELLS_ROW, D)
    grad_pooled = pick(grad_pooled, x) + flip(pick(grad_pooled, 1 - x), "x")
    grad_pooled = pick(grad_pooled, y) + flip(pick(grad_pooled, 1 - y), "y")
    gradient = grad_pooled / counts[:, None]

    parts = [None] * (6 * LAYERS)
    late = late_blocks = None
    vec_grads = [None] * LAYERS

    def gradients_of(low, high):
        rows = (8 * mat_rows * low, 8 * mat_rows * high)
        return PlaneReduce(*split_rows(parts, *rows, high - low, mat_rows, c), x, y)

    for layer in reversed(range(LAYERS)):
        span = slice(6 * layer, 6 * layer + 6)
        needed, more = (), lambda part: ()
        if short and layer == 1:

            def more(part):
                nonlocal late
                parts[9:12] = [(part, 1), (part, 2), (part, 3)]
                late = gradients_of(planes // 2, planes)
                return ()

        if short and layer == 0:
            late.one()
            needed = late.block
            more = lambda part: late.halves

        gradient, parts[span], vec_grads[layer] = layer_backward(
            gradient, stats[layer], store, places, vectors[layer], mats, layer, needed, more
        )

    grad_value = jnp.einsum("tb,td->bd", level_hot, gradient, precision=HIGHEST)
    grad_embedded = (math.sqrt(D) * gradient).astype(BF16)
    grad_plane, early = xy_gather(grad_embedded, 0)
    rest = gradients_of(0, planes // 2 if short else planes)
    rest.one()
    grad_col = dot_tn(hot, grad_plane.reshape(-1, D))
    grad_own = grad_col[:own_rows] + flip(grad_col[own_rows:].astype(BF16), "c").astype(F32)
    grad_own = grad_own + dot_tn(grad_pred[:, :own_rows], pooled_low)
    grad_own = grad_own.astype(BF16).reshape(planes, SLOT, D)[:, :rows_dev]
    if short:
        swaps = [z_swap(grad_own[k], k, planes) for k in range(1, planes)]
        grad_table = sum(term.astype(F32) for term in [grad_own[0], *swaps])
        blocks = jnp.concatenate([rest.two(grad_own), late.two(grad_own)])
        blocks = [lax.dynamic_index_in_dim(blocks, z ^ k, 0, False) for k in range(planes)]
        terms = [blocks[0]] + [z_swap(blocks[k], k, planes) for k in range(1, planes)]
        grad_matrices = sum(term.astype(F32) for term in terms)
    else:
        swaps = ()
        grad_table = jnp.sum(lax.all_to_all(grad_own, "z", 0, 0).astype(F32), axis=0)
        grad_matrices = owner_sum(rest.two(), 0, z, planes)

    small = jnp.concatenate([jnp.concatenate(vec_grads), grad_value])
    small = all_sum(small, planes)
    grad_vectors = small[: 6 * LAYERS].reshape(vectors.shape)
    grad_value = small[6 * LAYERS :]
    squares = jnp.sum(grad_matrices * grad_matrices) + jnp.sum(grad_table * grad_table)
    lanes = jnp.arange(128)[None, :]
    sums = jnp.where(lanes == 0, squares, jnp.where(lanes == 1, loss_part, 0.0))
    sums = small_sum(jnp.broadcast_to(sums, (8, 128)), x, y, z, planes)
    loss_sum = sums[0, 1]
    grad_norm = jnp.sqrt(sums[0, 0] + jnp.sum(small * small))
    factor = CLIP_NORM / grad_norm

    def update(weight, moment, average, grad_full):
        clipped = factor * grad_full
        moment_new = MOMENTUM * moment + clipped
        weight_new = weight - LEARN_RATE * (clipped + MOMENTUM * moment_new)
        return (
            moment_new,
            weight_new,
            AVERAGE_DECAY * average + (1.0 - AVERAGE_DECAY) * weight_new,
        )

    return (
        loss_sum,
        grad_norm,
        *update(matrices, matrices_mom, matrices_avg, grad_matrices),
        *update(vectors, vectors_mom, vectors_avg, grad_vectors),
        *update(value_table, value_mom, value_avg, grad_value),
        *update(gene_table, gene_mom, gene_avg, grad_table),
    )


def solution(mesh):
    devices = mesh.devices
    fine = Mesh(devices.reshape(devices.shape[0] // 4, 2, 2, devices.shape[1]), ("z", "x", "c", "y"))
    dp = ("z", "x", "c")
    every = ("z", "x", "c", "y")
    weights = (P(every, None), P(), P(), P(every, None))
    in_specs = (P(dp, None),) * 3 + (P(dp, None, None), P(None, every)) + weights * 3
    out_specs = (P(), P()) + (P(every, None),) * 3 + (P(),) * 6 + (P(every, None),) * 3
    return jax.shard_map(local, mesh=fine, in_specs=in_specs, out_specs=out_specs, check_vma=False)
```
